32 devices in a mesh: by: 4 (over x, core), bx: 8 (over z, y).
Axes of the slice: x: 2, y: 2, z: 4, core: 2. Of those that a mesh axis runs over, the one named last changes fastest.
Arguments:
- tracer_one: float32 [18, 256, 2048], P(None, 'by', 'bx'), may hold values from -6 to 6
- tracer_two: float32 [18, 256, 2048], P(None, 'by', 'bx'), may hold values from -6 to 6
- east_flow: bfloat16 [18, 256, 2048], P(None, 'by', 'bx'), may hold values from -0.3984375 to 0.3984375
- north_flow: bfloat16 [18, 256, 2048], P(None, 'by', 'bx'), may hold values from -0.3984375 to 0.3984375
- depth_levels: int32 [256, 2048], P('by', 'bx'), may hold values from 0 to 18
- side_mix: float32 [18], replicated, may hold values from 0.02 to 0.2
- vert_mix: float32 [18], replicated, may hold values from 0.01 to 0.3
- thickness: float32 [18], replicated, may hold values from 0.1 to 0.4
- corner_depth: float32 [256, 2048], P('by', 'bx'), may hold values from 0.5 to 4
- diagonal: float32 [256, 2048], P('by', 'bx'), may hold values from 0.05 to 0.5
Outputs:
- new_one: float32 [18, 256, 2048], P(None, 'by', 'bx')
- new_two: float32 [18, 256, 2048], P(None, 'by', 'bx')
- surface: float32 [256, 2048], P('by', 'bx')
The draws below stay inside these ranges and needn't reach their ends.
All inputs are finite; a program needn't handle non-finite values.
Results may differ from the reference program's by a relative error of at most 0.0003.
Values may be sent and summed in bfloat16 or wider, within the bound.
A program may use at most 192 MiB of HBM per device.

```python
import math
import jax
import jax.numpy as jnp
from jax import lax

LEV = 18
ITERS = 3
NX = 2048
NY = 256


def touch_ends(result, stream_key, least, top_value):
    longest = result.shape.index(max(result.shape))
    spots = []
    for shift in (0, 1):
        where = [jax.random.randint(jax.random.fold_in(stream_key, axis), (), 0, length) for axis, length in enumerate(result.shape)]
        where[longest] = (where[longest] + shift) % result.shape[longest]
        spots.append(tuple(where))
    return result.at[spots[0]].set(least).at[spots[1]].set(top_value)


def shard_levels(own_key, dims, pieces, smallest, high):
    factor_of = 1.0
    for position, parts in pieces:
        heights = jax.random.uniform(jax.random.fold_in(jax.random.fold_in(own_key, 6), position), (parts,), jnp.float32, smallest / len(pieces), high / len(pieces))
        factor_of = factor_of * jnp.repeat(jnp.exp(heights), dims[position] // parts).reshape((-1,) + (1,) * (len(dims) - 1 - position))
    return factor_of


def gaussian(key, extent, deviation, bound, pieces=(), kind=jnp.bfloat16):
    drawn = deviation * jax.random.normal(key, extent, jnp.float32)
    if pieces:
        drawn = drawn * shard_levels(key, extent, pieces, -0.22, 0.18)
    return jnp.clip(drawn, -bound, bound).astype(kind)


def setup_inputs(seed: int = 0) -> dict:
    keys = jax.random.split(jax.random.key(seed), 11)
    return {
        "tracer_one": gaussian(keys[0], (LEV, NY, NX), 1.0, 6.0, ((1, 4), (2, 8)), jnp.float32),
        "tracer_two": gaussian(keys[1], (LEV, NY, NX), 1.0, 6.0, ((1, 4), (2, 8)), jnp.float32),
        "east_flow": jnp.clip(jax.random.uniform(keys[2], (LEV, NY, NX), jnp.float32, -0.3984375, 0.3984375) * shard_levels(keys[2], (LEV, NY, NX), ((1, 4), (2, 8)), -0.4, 0.0), -0.3984375, 0.3984375).astype(jnp.bfloat16),
        "north_flow": jnp.clip(jax.random.uniform(keys[3], (LEV, NY, NX), jnp.float32, -0.3984375, 0.3984375) * shard_levels(keys[3], (LEV, NY, NX), ((1, 4), (2, 8)), -0.4, 0.0), -0.3984375, 0.3984375).astype(jnp.bfloat16),
        "depth_levels": touch_ends(jax.random.randint(keys[4], (NY, NX), 0, LEV + 1), jax.random.fold_in(keys[4], 1), 0, LEV).astype(jnp.int32),
        "side_mix": jnp.clip(jnp.exp(jax.random.uniform(keys[5], (LEV,), jnp.float32, math.log(0.02), math.log(0.2))), 0.02, 0.2),
        "vert_mix": jnp.clip(jnp.exp(jax.random.uniform(keys[6], (LEV,), jnp.float32, math.log(0.01), math.log(0.3))), 0.01, 0.3),
        "thickness": jnp.clip(jnp.exp(jax.random.uniform(keys[7], (LEV,), jnp.float32, math.log(0.1), math.log(0.4))), 0.1, 0.4),
        "corner_depth": jnp.clip(jnp.exp(math.log(4.0) - 2.0794415 * jax.random.uniform(keys[8], (NY, NX), jnp.float32) ** shard_levels(keys[8], (NY, NX), ((0, 4), (1, 8)), -0.2, 0.2)), 0.5, 4.0),
        "diagonal": jnp.clip(jnp.exp(math.log(0.5) - 2.3025851 * jax.random.uniform(keys[9], (NY, NX), jnp.float32) ** shard_levels(keys[9], (NY, NX), ((0, 4), (1, 8)), -0.2, 0.2)), 0.05, 0.5),
    }


def pad_field(field):
    field = jnp.pad(field, [(0, 0)] * (field.ndim - 1) + [(1, 1)], mode="wrap")
    return jnp.pad(field, [(0, 0)] * (field.ndim - 2) + [(1, 1), (0, 0)])


def horizontal(padded, side):
    tracers = padded[0:2]
    east_vel = padded[2]
    north_vel = padded[3]
    wet_pad = padded[4]
    left = tracers[..., 1:-1, :-1]
    right = tracers[..., 1:-1, 1:]
    face_east = wet_pad[..., 1:-1, :-1] * wet_pad[..., 1:-1, 1:]
    east = (east_vel[..., 1:-1, :-1] * 0.5 * (left + right) - side * (right - left)) * face_east
    lower = tracers[..., :-1, 1:-1]
    upper = tracers[..., 1:, 1:-1]
    face_north = wet_pad[..., :-1, 1:-1] * wet_pad[..., 1:, 1:-1]
    north = (north_vel[..., :-1, 1:-1] * 0.5 * (lower + upper) - side * (upper - lower)) * face_north
    return -(east[..., 1:] - east[..., :-1]) - (north[..., 1:, :] - north[..., :-1, :])


def vertical(tracers, wet, vert_mix):
    falling = vert_mix[:-1, None, None] * (tracers[:, 1:] - tracers[:, :-1]) * wet[1:]
    zeros = jnp.zeros_like(tracers[:, :1])
    padded = jnp.concatenate([zeros, falling, zeros], axis=1)
    return padded[:, 1:] - padded[:, :-1]


def corner_operator(extended, depth_ext, field, diagonal):
    cell_a = extended[:-1, :-1]
    cell_b = extended[:-1, 1:]
    cell_c = extended[1:, :-1]
    cell_d = extended[1:, 1:]
    grad_x = 0.5 * ((cell_b + cell_d) - (cell_a + cell_c))
    grad_y = 0.5 * ((cell_c + cell_d) - (cell_a + cell_b))
    flux_x = depth_ext * grad_x
    flux_y = depth_ext * grad_y
    plus = flux_x + flux_y
    minus = flux_x - flux_y
    return (diagonal * field - 0.5 * plus[1:, 1:] + 0.5 * minus[1:, :-1]
            - 0.5 * minus[:-1, 1:] + 0.5 * plus[:-1, :-1])


def chron_gear(forcing, operate, totals):
    surface = jnp.zeros_like(forcing)
    residual = forcing
    image = operate(residual)
    norm_now, product = totals(residual * residual, residual * image)
    alpha = norm_now / product
    direction, along = residual, image
    for step in range(ITERS):
        surface = surface + alpha * direction
        residual = residual - alpha * along
        if step + 1 < ITERS:
            image = operate(residual)
            norm_next, product = totals(residual * residual, residual * image)
            ratio = norm_next / norm_now
            alpha = norm_next / (product - ratio * norm_next / alpha)
            direction = residual + ratio * direction
            along = image + ratio * along
            norm_now = norm_next
    return surface


def global_totals(first, second):
    return jnp.sum(first), jnp.sum(second)


def reference(tracer_one, tracer_two, east_flow, north_flow, depth_levels, side_mix, vert_mix, thickness, corner_depth, diagonal):
    levels = lax.broadcasted_iota(jnp.int32, tracer_one.shape, 0)
    wet = (levels < depth_levels[None]).astype(jnp.float32)

    def level_step(items):
        first, second, east, north, wet_level, side = items
        stacked = jnp.stack([first, second, east.astype(jnp.float32), north.astype(jnp.float32), wet_level])
        return horizontal(pad_field(stacked), side)

    change = lax.map(level_step, (tracer_one, tracer_two, east_flow, north_flow, wet, side_mix))
    change = jnp.transpose(change, (1, 0, 2, 3))
    tracers = jnp.stack([tracer_one, tracer_two])
    updated = wet * (tracers + change + vertical(tracers, wet, vert_mix))
    forcing = jnp.sum(thickness[:, None, None] * (updated[0] - 0.5 * updated[1]), axis=0)
    depth = corner_depth * (depth_levels > 0).astype(jnp.float32)
    depth_ext = pad_field(depth)[:-1, :-1]

    def operate(field):
        return corner_operator(pad_field(field), depth_ext, field, diagonal)

    surface = chron_gear(forcing, operate, global_totals)
    return updated[0], updated[1], surface
```

```python
import functools

import jax
import jax.numpy as jnp
from jax import lax
from jax.experimental import pallas as pl
from jax.experimental.pallas import tpu as pltpu
from jax.sharding import PartitionSpec as P

ITERS = 3
SHIFT = 3.0
CHUNK = 16
LANES = 128
MESH = pl.DeviceIdType.MESH
f32 = jnp.float32
SIDES = ((1, 0), (-1, 0), (0, 1), (0, -1), (1, 1), (1, -1), (-1, 1), (-1, -1))


def iterate_weights(moments):
    def add(a, b, scale):
        longer = max(len(a), len(b))
        out = []
        for n in range(longer):
            if n >= len(a):
                out.append(scale * b[n])
            elif n >= len(b):
                out.append(a[n])
            else:
                out.append(a[n] + scale * b[n])
        return out

    def operate(a):
        shifted = [SHIFT * x for x in a] + [None]
        for n, x in enumerate(a):
            shifted[n + 1] = x if shifted[n + 1] is None else shifted[n + 1] + x
        return shifted

    def dot(a, b):
        total = None
        for i, x in enumerate(a):
            for j, y in enumerate(b):
                term = x * y * moments[i + j]
                total = term if total is None else total + term
        return total

    residual = [jnp.ones_like(moments[0])]
    image = operate(residual)
    now = dot(residual, residual)
    alpha = now / dot(residual, image)
    direction, along = residual, image
    surface = [jnp.zeros_like(moments[0])]
    for step in range(ITERS):
        surface = add(surface, direction, alpha)
        if step + 1 < ITERS:
            residual = add(residual, along, -alpha)
            image = operate(residual)
            new = dot(residual, residual)
            product = dot(residual, image)
            ratio = new / now
            alpha = new / (product - ratio * new / alpha)
            direction = add(residual, direction, ratio)
            along = add(image, along, ratio)
            now = new
    return surface


def kernel(
    nby, nbx, nlev,
    side, vert, thick, t1h, t2h, uh, vh, levh, cdh, dgh,
    o1h, o2h, surf,
    t, u, v, levi, o, row_up, row_dn, got_dn, got_up, col_rt, col_lf, got_lf, got_rt,
    flx, fw, fld, h_up, h_dn, h_rt, h_lf, h_cn, v1r, v2r, mom, gath,
    load_sem, out_sem, send_a, recv_a, send_b, recv_b, send_c, recv_c, gsend, grecv,
):
    by, bx = lax.axis_index("by"), lax.axis_index("bx")
    total = nby * nbx
    me = by * nbx + bx
    ny, nx = fld.shape[1], fld.shape[2]

    loads = [
        pltpu.make_async_copy(levh, levi, load_sem.at[4]),
        pltpu.make_async_copy(cdh, fld.at[1], load_sem.at[5]),
        pltpu.make_async_copy(dgh, fld.at[2], load_sem.at[6]),
        pltpu.make_async_copy(t1h, t.at[0], load_sem.at[0]),
        pltpu.make_async_copy(t2h, t.at[1], load_sem.at[1]),
        pltpu.make_async_copy(uh, u, load_sem.at[2]),
        pltpu.make_async_copy(vh, v, load_sem.at[3]),
    ]
    for copy in loads:
        copy.start()

    def other(off):
        who = lax.rem(me + off, total)
        return (who // nbx, lax.rem(who, nbx))

    barrier = pltpu.get_barrier_semaphore()

    def greet(off, _):
        pl.semaphore_signal(barrier, inc=1, device_id=other(off), device_id_type=MESH)
        return 0

    lax.fori_loop(1, total, greet, 0)

    def neighbour(dy, dx):
        return (lax.rem(by + dy + nby, nby), lax.rem(bx + dx + nbx, nbx))

    up_ok = jnp.where(by < nby - 1, 1.0, 0.0).astype(f32)
    dn_ok = jnp.where(by > 0, 1.0, 0.0).astype(f32)

    for copy in loads[:3]:
        copy.wait()
    levels = levi[...]
    levf = levels.astype(f32)
    fld[1] = fld[1] * jnp.where(levels > 0, 0.5, 0.0).astype(f32)
    fld[2] = fld[2] - SHIFT
    for copy in loads[3:]:
        copy.wait()

    lane = lax.broadcasted_iota(jnp.int32, (ny, LANES), 1)
    row_up[pl.ds(72, 8), :] = jnp.broadcast_to(levf[ny - 1 : ny], (8, nx))
    row_dn[pl.ds(72, 8), :] = jnp.broadcast_to(levf[0:1], (8, nx))

    def pack(k, carry):
        right, left = carry
        for c in range(2):
            row_up[pl.ds(24 * c + k, 1), :] = t[c, k, ny - 1 : ny, :]
            row_dn[pl.ds(24 * c + k, 1), :] = t[c, k, 0:1, :]
            place = 32 * c + k
            right = jnp.where(lane == place, pltpu.roll(t[c, k, :, nx - LANES :], place + 1, 1), right)
            left = jnp.where(lane == place, pltpu.roll(t[c, k, :, :LANES], place, 1), left)
        row_up[pl.ds(48 + k, 1), :] = v[k, ny - 16 :, :].astype(f32)[15:16]
        right = jnp.where(lane == 64 + k, pltpu.roll(u[k, :, nx - LANES :].astype(f32), 65 + k, 1), right)
        return right, left

    first = jnp.zeros((ny, LANES), f32)
    right, left = lax.fori_loop(0, nlev, pack, (first, first))
    col_rt[...] = jnp.where(lane == 96, pltpu.roll(levf[:, nx - LANES :], 97, 1), right)
    col_lf[...] = jnp.where(lane == 96, pltpu.roll(levf[:, :LANES], 96, 1), left)

    pl.semaphore_wait(barrier, total - 1)

    def send(src, dst, ssem, rsem, to):
        copy = pltpu.make_async_remote_copy(
            src_ref=src, dst_ref=dst, send_sem=ssem, recv_sem=rsem, device_id=to, device_id_type=MESH
        )
        copy.start()
        return copy

    edge = [
        send(row_up, got_dn, send_a.at[0], recv_a.at[0], neighbour(1, 0)),
        send(row_dn, got_up, send_a.at[1], recv_a.at[1], neighbour(-1, 0)),
        send(col_rt, got_lf, send_a.at[2], recv_a.at[2], neighbour(0, 1)),
        send(col_lf, got_rt, send_a.at[3], recv_a.at[3], neighbour(0, -1)),
    ]

    def rim(which, ssem, rsem):
        copies = []
        for n, (dy, dx) in enumerate(SIDES):
            rows = pl.ds(0, ny) if dy == 0 else (pl.ds(ny - 8, 8) if dy > 0 else pl.ds(0, 8))
            cols = pl.ds(0, nx) if dx == 0 else (pl.ds(nx - LANES, LANES) if dx > 0 else pl.ds(0, LANES))
            place = {0: h_dn, 1: h_up, 2: h_lf, 3: h_rt}.get(n)
            dst = h_cn.at[n - 4, which] if place is None else place.at[which]
            copies.append(send(fld.at[which, rows, cols], dst, ssem.at[n], rsem.at[n], neighbour(dy, dx)))
        return copies

    rim_fixed = rim(pl.ds(1, 2), send_b, recv_b)

    for copy in edge:
        copy.wait_recv()

    k_sub = lax.broadcasted_iota(jnp.int32, (24, nx), 0)
    k_lane = lax.rem(lane, 32)
    side_sub = jnp.zeros((24, nx), f32)
    side_lane = jnp.zeros((ny, LANES), f32)
    for k in range(nlev):
        side_sub = jnp.where(k_sub == k, side[k], side_sub)
        side_lane = jnp.where(k_lane == k, side[k], side_lane)
    lowest = jnp.minimum(got_dn[72:73, :] * dn_ok, levf[0:1])
    open_dn = k_sub.astype(f32) < lowest
    half = 0.5 * got_dn[48:72, :]
    for c in range(2):
        flux = (half + side_sub) * got_dn[24 * c : 24 * c + 24, :] + (half - side_sub) * row_dn[24 * c : 24 * c + 24, :]
        flx[c] = jnp.where(open_dn, flux, 0.0)
    came = got_lf[...]
    half = 0.5 * jnp.where(lane < 32, pltpu.roll(came, 64, 1), pltpu.roll(came, 96, 1))
    lowest = jnp.minimum(came[:, 96:97], levf[:, 0:1])
    flux = (half + side_lane) * came + (half - side_lane) * col_lf[...]
    fw[...] = jnp.where(k_lane.astype(f32) < lowest, flux, 0.0)

    lane_c = lax.broadcasted_iota(jnp.int32, (CHUNK, LANES), 1)
    sub_c = lax.broadcasted_iota(jnp.int32, (CHUNK, nx), 0)

    def at_last_lane(whole, tile):
        return jnp.concatenate([whole[:, : nx - LANES], jnp.where(lane_c == LANES - 1, tile, whole[:, nx - LANES :])], axis=1)

    def at_first_lane(whole, tile):
        return jnp.concatenate([jnp.where(lane_c == 0, tile, whole[:, :LANES]), whole[:, LANES:]], axis=1)

    for r in range(0, ny, CHUNK):
        rows = slice(r, r + CHUNK)
        lev = levf[rows]
        lev_rt = at_last_lane(pltpu.roll(lev, nx - 1, 1), jnp.broadcast_to(got_rt[rows, 96:97], (CHUNK, LANES)))
        above = levf[r + CHUNK : r + CHUNK + 1] if r + CHUNK < ny else got_up[72:73, :] * up_ok
        lev_up = jnp.where(sub_c == CHUNK - 1, above, pltpu.roll(lev, CHUNK - 1, 0))
        open_e = jnp.minimum(lev, lev_rt)
        open_n = jnp.minimum(lev, lev_up)

        def level(k, carry, r=r, rows=rows, lev=lev, open_e=open_e, open_n=open_n):
            falls, force = carry
            kf = k.astype(f32)
            s = side[k]
            hu = 0.5 * u[k, rows, :].astype(f32)
            hv = 0.5 * v[k, rows, :].astype(f32)
            in_e, in_n = kf < open_e, kf < open_n
            pe, qe = jnp.where(in_e, hu + s, 0.0), jnp.where(in_e, hu - s, 0.0)
            pn, qn = jnp.where(in_n, hv + s, 0.0), jnp.where(in_n, hv - s, 0.0)
            wet = kf < lev
            fall_w = jnp.where(kf + 1.0 < lev, vert[k], 0.0)
            below = jnp.minimum(k + 1, nlev - 1)
            rt, lf = got_rt[rows, :], fw[rows, :]
            news, next_falls = [], []
            for c in range(2):
                here = t[c, k, rows, :]
                right = at_last_lane(pltpu.roll(here, nx - 1, 1), pltpu.roll(rt, 127 - 32 * c - k, 1))
                top = t[c, k, r + CHUNK : r + CHUNK + 1, :] if r + CHUNK < ny else got_up[pl.ds(24 * c + k, 1), :]
                upper = jnp.where(sub_c == CHUNK - 1, top, pltpu.roll(here, CHUNK - 1, 0))
                east = pe * here + qe * right
                north = pn * here + qn * upper
                west = at_first_lane(pltpu.roll(east, 1, 1), pltpu.roll(lf, lax.rem(128 - 32 * c - k, 128), 1))
                south = jnp.where(sub_c == 0, flx[c, pl.ds(k, 1), :], pltpu.roll(north, 1, 0))
                if r + CHUNK < ny:
                    flx[c, pl.ds(k, 1), :] = north[CHUNK - 1 :]
                fall = fall_w * (t[c, below, rows, :] - here)
                new = jnp.where(wet, here + (west - east) + (south - north) + (fall - falls[c]), 0.0)
                o[c, k, rows, :] = new
                news.append(new)
                next_falls.append(fall)
            force = force + thick[k] * (news[0] - 0.5 * news[1])
            return tuple(next_falls), force

        zero = jnp.zeros((CHUNK, nx), f32)
        _, force = lax.fori_loop(0, nlev, level, ((zero, zero), zero))
        fld[0, rows, :] = force

    outs = [
        pltpu.make_async_copy(o.at[0], o1h, out_sem.at[0]),
        pltpu.make_async_copy(o.at[1], o2h, out_sem.at[1]),
    ]
    rim_force = rim(0, send_c, recv_c)
    for copy in outs:
        copy.start()

    sub8 = lax.broadcasted_iota(jnp.int32, (8, nx), 0) < 4
    sub8c = sub8[:, :LANES]
    lane8 = lax.broadcasted_iota(jnp.int32, (8, LANES), 1) < 64
    lane64 = lane < 64
    row = lax.broadcasted_iota(jnp.int32, (ny + 8, nx + LANES), 0)
    mask = jnp.where(row < ny, 1.0, jnp.where(row < ny + 4, up_ok, dn_ok)).astype(f32)

    def widened(n):
        beside = jnp.where(lane64, h_rt[n], h_lf[n])
        ends = jnp.where(sub8, h_up[n], h_dn[n])
        corner = jnp.where(
            sub8c, jnp.where(lane8, h_cn[3, n], h_cn[2, n]), jnp.where(lane8, h_cn[1, n], h_cn[0, n])
        )
        top = jnp.concatenate([fld[n], beside], axis=1)
        bottom = jnp.concatenate([ends, corner], axis=1)
        return jnp.concatenate([top, bottom], axis=0) * mask

    for copy in rim_fixed:
        copy.wait_recv()
    depth, diag = widened(1), widened(2)
    for copy in rim_force:
        copy.wait_recv()
    tall, wide = ny + 8, nx + LANES

    def operate(a):
        b = pltpu.roll(a, wide - 1, 1)
        cc = pltpu.roll(a, tall - 1, 0)
        d = pltpu.roll(b, tall - 1, 0)
        p = depth * (d - a)
        q = depth * (b - cc)
        return (diag * a - p + pltpu.roll(q, 1, 1) + pltpu.roll(pltpu.roll(p, 1, 1) - q, 1, 0)) * mask

    def moment(a, b):
        prod = a[:ny, :nx] * b[:ny, :nx]
        prod = jnp.sum(prod.reshape(ny // 8, 8, nx), axis=0)
        prod = sum(prod[:, n : n + LANES] for n in range(0, nx, LANES))
        return jnp.sum(prod, axis=0, keepdims=True)

    w0 = widened(0)
    w1 = operate(w0)
    w2 = operate(w1)
    w3 = operate(w2)
    v1r[...] = w1[:ny, :nx]
    v2r[...] = w2[:ny, :nx]
    pairs = ((w0, w0), (w0, w1), (w1, w1), (w1, w2), (w2, w2), (w2, w3))
    mom[...] = jnp.concatenate([moment(a, b) for a, b in pairs] + [jnp.zeros((2, LANES), f32)], axis=0)

    def tell(off, _):
        send(mom, gath.at[me], gsend, grecv, other(off))
        return 0

    lax.fori_loop(1, total, tell, 0)
    gath[me] = mom[...]
    for copy in edge + rim_fixed + rim_force:
        copy.wait_send()
    for copy in outs:
        copy.wait()
    every = gath.at[pl.ds(0, total - 1)]
    pltpu.make_async_copy(every, every, grecv).wait()
    sums = jnp.sum(jnp.sum(gath[...], axis=0), axis=1, keepdims=True)
    weights = iterate_weights([sums[n : n + 1] for n in range(6)])
    surf[...] = weights[0] * fld[0] + weights[1] * v1r[...] + weights[2] * v2r[...]
    pltpu.make_async_copy(every, every, gsend).wait()


def on_device(nby, nbx, t1, t2, u, v, lev, side, vert, thick, cd, dg):
    nlev, ny, nx = t1.shape
    anywhere = pl.BlockSpec(memory_space=pl.ANY)
    scalars = pl.BlockSpec(memory_space=pltpu.SMEM)
    vmem = pltpu.VMEM
    dma = pltpu.SemaphoreType.DMA
    cells = nlev * ny * nx
    return pl.pallas_call(
        functools.partial(kernel, nby, nbx, nlev),
        out_shape=(
            jax.ShapeDtypeStruct(t1.shape, f32),
            jax.ShapeDtypeStruct(t1.shape, f32),
            jax.ShapeDtypeStruct((ny, nx), f32),
        ),
        in_specs=[scalars] * 3 + [anywhere] * 7,
        out_specs=(anywhere, anywhere, pl.BlockSpec(memory_space=vmem)),
        scratch_shapes=[
            vmem((2, nlev, ny, nx), f32),
            vmem((nlev, ny, nx), u.dtype),
            vmem((nlev, ny, nx), v.dtype),
            vmem((ny, nx), jnp.int32),
            vmem((2, nlev, ny, nx), f32),
            vmem((80, nx), f32),
            vmem((80, nx), f32),
            vmem((80, nx), f32),
            vmem((80, nx), f32),
            vmem((ny, LANES), f32),
            vmem((ny, LANES), f32),
            vmem((ny, LANES), f32),
            vmem((ny, LANES), f32),
            vmem((2, 24, nx), f32),
            vmem((ny, LANES), f32),
            vmem((3, ny, nx), f32),
            vmem((3, 8, nx), f32),
            vmem((3, 8, nx), f32),
            vmem((3, ny, LANES), f32),
            vmem((3, ny, LANES), f32),
            vmem((4, 3, 8, LANES), f32),
            vmem((ny, nx), f32),
            vmem((ny, nx), f32),
            vmem((8, LANES), f32),
            vmem((nby * nbx, 8, LANES), f32),
            dma((7,)),
            dma((2,)),
            dma((4,)),
            dma((4,)),
            dma((8,)),
            dma((8,)),
            dma((8,)),
            dma((8,)),
            dma,
            dma,
        ],
        compiler_params=pltpu.CompilerParams(
            collective_id=0, has_side_effects=True, vmem_limit_bytes=40 * 2**20
        ),
        cost_estimate=pl.CostEstimate(flops=60 * cells, bytes_accessed=20 * cells, transcendentals=0),
    )(side, vert, thick, t1, t2, u, v, lev, cd, dg)


def solution(mesh):
    def body(t1, t2, u, v, lev, side, vert, thick, cd, dg):
        return on_device(mesh.shape["by"], mesh.shape["bx"], t1, t2, u, v, lev, side, vert, thick, cd, dg)

    block, plane = P(None, "by", "bx"), P("by", "bx")
    return jax.shard_map(
        body,
        mesh=mesh,
        in_specs=(block, block, block, block, plane, P(), P(), P(), plane, plane),
        out_specs=(block, block, plane),
        check_vma=False,
    )
```

```python
import functools

import jax
import jax.numpy as jnp
from jax import lax
from jax.experimental import pallas as pl
from jax.experimental.pallas import tpu as pltpu
from jax.sharding import PartitionSpec as P

ITERS = 3
SHIFT = 3.0
CHUNK = 16
UNROLL = 2
VMEM_MIB = 62
LANES = 128
MESH = pl.DeviceIdType.MESH
f32 = jnp.float32
SIDES = ((1, 0), (-1, 0), (0, 1), (0, -1), (1, 1), (1, -1), (-1, 1), (-1, -1))


def iterate_weights(moments):
    def add(a, b, scale):
        longer = max(len(a), len(b))
        out = []
        for n in range(longer):
            if n >= len(a):
                out.append(scale * b[n])
            elif n >= len(b):
                out.append(a[n])
            else:
                out.append(a[n] + scale * b[n])
        return out

    def operate(a):
        shifted = [SHIFT * x for x in a] + [None]
        for n, x in enumerate(a):
            shifted[n + 1] = x if shifted[n + 1] is None else shifted[n + 1] + x
        return shifted

    def dot(a, b):
        total = None
        for i, x in enumerate(a):
            for j, y in enumerate(b):
                term = x * y * moments[i + j]
                total = term if total is None else total + term
        return total

    residual = [jnp.ones_like(moments[0])]
    image = operate(residual)
    now = dot(residual, residual)
    alpha = now / dot(residual, image)
    direction, along = residual, image
    surface = [jnp.zeros_like(moments[0])]
    for step in range(ITERS):
        surface = add(surface, direction, alpha)
        if step + 1 < ITERS:
            residual = add(residual, along, -alpha)
            image = operate(residual)
            new = dot(residual, residual)
            product = dot(residual, image)
            ratio = new / now
            alpha = new / (product - ratio * new / alpha)
            direction = add(residual, direction, ratio)
            along = add(image, along, ratio)
            now = new
    return surface


def kernel(
    nby, nbx, nlev,
    sideh, verth, thickh, t1h, t2h, uh, vh, levh, cdh, dgh,
    o1h, o2h, surf,
    side, vert, thick, t, u, v, levi, o, row_up, row_dn, got_dn, got_up, col_rt, col_lf, got_lf, got_rt,
    lv, fall_in, fld, h_up, h_dn, h_rt, h_lf, h_cn, v1r, v2r, mom, gath,
    load_sem, out_sem, send_a, recv_a, send_b, recv_b, send_c, recv_c, gsend, grecv,
):
    by, bx = lax.axis_index("by"), lax.axis_index("bx")
    total = nby * nbx
    me = by * nbx + bx
    ny, nx = fld.shape[1], fld.shape[2]

    loads = [
        pltpu.make_async_copy(sideh, side, load_sem.at[7]),
        pltpu.make_async_copy(verth, vert, load_sem.at[8]),
        pltpu.make_async_copy(thickh, thick, load_sem.at[9]),
        pltpu.make_async_copy(levh, levi, load_sem.at[4]),
        pltpu.make_async_copy(t1h, t.at[0], load_sem.at[0]),
        pltpu.make_async_copy(t2h, t.at[1], load_sem.at[1]),
        pltpu.make_async_copy(uh, u, load_sem.at[2]),
        pltpu.make_async_copy(vh, v, load_sem.at[3]),
        pltpu.make_async_copy(cdh, fld.at[1], load_sem.at[5]),
        pltpu.make_async_copy(dgh, fld.at[2], load_sem.at[6]),
    ]
    for copy in loads:
        copy.start()

    def neighbour(dy, dx):
        y, x = by + dy % nby, bx + dx % nbx
        return (jnp.where(y >= nby, y - nby, y), jnp.where(x >= nbx, x - nbx, x))

    others = [(dy, dx) for dy in range(nby) for dx in range(nbx)][1:]
    barrier = pltpu.get_barrier_semaphore()
    for dy, dx in others:
        pl.semaphore_signal(barrier, inc=1, device_id=neighbour(dy, dx), device_id_type=MESH)

    up_ok = jnp.where(by < nby - 1, 1.0, 0.0).astype(f32)
    dn_ok = jnp.where(by > 0, 1.0, 0.0).astype(f32)

    for copy in loads[:4]:
        copy.wait()
    levels = levi[...]
    levf = levels.astype(f32)

    lane = lax.broadcasted_iota(jnp.int32, (ny, LANES), 1)
    row_up[pl.ds(72, 8), :] = jnp.broadcast_to(levf[ny - 1 : ny], (8, nx))
    row_dn[pl.ds(72, 8), :] = jnp.broadcast_to(levf[0:1], (8, nx))
    right = jnp.where(lane == 96, pltpu.roll(levf[:, nx - LANES :], 97, 1), 0.0)
    left = jnp.where(lane == 96, pltpu.roll(levf[:, :LANES], 96, 1), 0.0)
    for c in range(2):
        loads[4 + c].wait()
        for k in range(nlev):
            row_up[24 * c + k : 24 * c + k + 1, :] = t[c, k, ny - 1 : ny, :]
            row_dn[24 * c + k : 24 * c + k + 1, :] = t[c, k, 0:1, :]
            place = 32 * c + k
            right = jnp.where(lane == place, pltpu.roll(t[c, k, :, nx - LANES :], place + 1, 1), right)
            tile = t[c, k, :, :LANES]
            left = jnp.where(lane == place, pltpu.roll(tile, place, 1) if place else tile, left)
    loads[6].wait()
    for k in range(nlev):
        right = jnp.where(lane == 64 + k, pltpu.roll(u[k, :, nx - LANES :].astype(f32), 65 + k, 1), right)
    loads[7].wait()
    for k in range(nlev):
        row_up[48 + k : 49 + k, :] = v[k, ny - 16 :, :].astype(f32)[15:16]
    col_rt[...] = right
    col_lf[...] = left

    pl.semaphore_wait(barrier, total - 1)

    def send(src, dst, ssem, rsem, to):
        copy = pltpu.make_async_remote_copy(
            src_ref=src, dst_ref=dst, send_sem=ssem, recv_sem=rsem, device_id=to, device_id_type=MESH
        )
        copy.start()
        return copy

    edge = [
        send(row_up, got_dn, send_a.at[0], recv_a.at[0], neighbour(1, 0)),
        send(row_dn, got_up, send_a.at[1], recv_a.at[1], neighbour(-1, 0)),
        send(col_rt, got_lf, send_a.at[2], recv_a.at[2], neighbour(0, 1)),
        send(col_lf, got_rt, send_a.at[3], recv_a.at[3], neighbour(0, -1)),
    ]

    def rim(which, ssem, rsem):
        copies = []
        for n, (dy, dx) in enumerate(SIDES):
            rows = pl.ds(0, ny) if dy == 0 else (pl.ds(ny - 8, 8) if dy > 0 else pl.ds(0, 8))
            cols = pl.ds(0, nx) if dx == 0 else (pl.ds(nx - LANES, LANES) if dx > 0 else pl.ds(0, LANES))
            place = {0: h_dn, 1: h_up, 2: h_lf, 3: h_rt}.get(n)
            dst = h_cn.at[n - 4, which] if place is None else place.at[which]
            copies.append(send(fld.at[which, rows, cols], dst, ssem.at[n], rsem.at[n], neighbour(dy, dx)))
        return copies

    for copy in loads[8:]:
        copy.wait()
    fld[1] = fld[1] * jnp.where(levels > 0, 0.5, 0.0).astype(f32)
    fld[2] = fld[2] - SHIFT
    rim_fixed = rim(pl.ds(1, 2), send_b, recv_b)

    sub_c = lax.broadcasted_iota(jnp.int32, (CHUNK, nx), 0)
    lane_c = lax.broadcasted_iota(jnp.int32, (CHUNK, nx), 1)
    for r in range(0, ny, CHUNK):
        rows = slice(r, r + CHUNK)
        lev = levf[rows]
        lev_rt = jnp.where(lane_c == nx - 1, 0.0, pltpu.roll(lev, nx - 1, 1))
        above = levf[r + CHUNK : r + CHUNK + 1] if r + CHUNK < ny else 0.0
        lev_up = jnp.where(sub_c == CHUNK - 1, above, pltpu.roll(lev, CHUNK - 1, 0))
        lv[0, rows, :] = lev
        lv[1, rows, :] = jnp.minimum(lev, lev_rt)
        lv[2, rows, :] = jnp.minimum(lev, lev_up)
    fall_in[...] = jnp.zeros_like(fall_in)
    fld[0] = jnp.zeros((ny, nx), f32)

    def level(k, _):
        kf = k.astype(f32)
        s, vk, tk = side[k], vert[k], thick[k]
        below = jnp.minimum(k + 1, nlev - 1)
        last = [0.0, 0.0]
        for r in range(0, ny, CHUNK):
            rows = slice(r, r + CHUNK)
            lev = lv[0, rows, :]
            hu = 0.5 * u[k, rows, :].astype(f32)
            hv = 0.5 * v[k, rows, :].astype(f32)
            in_e, in_n = kf < lv[1, rows, :], kf < lv[2, rows, :]
            pe, qe = jnp.where(in_e, hu + s, 0.0), jnp.where(in_e, hu - s, 0.0)
            pn, qn = jnp.where(in_n, hv + s, 0.0), jnp.where(in_n, hv - s, 0.0)
            wet = kf < lev
            fall_w = jnp.where(kf + 1.0 < lev, vk, 0.0)
            news = []
            for c in range(2):
                here = t[c, k, rows, :]
                upper = pltpu.roll(here, CHUNK - 1, 0)
                if r + CHUNK < ny:
                    upper = jnp.where(sub_c == CHUNK - 1, t[c, k, r + CHUNK : r + CHUNK + 1, :], upper)
                east = pe * here + qe * pltpu.roll(here, nx - 1, 1)
                north = pn * here + qn * upper
                south = jnp.where(sub_c == 0, last[c], pltpu.roll(north, 1, 0))
                last[c] = north[CHUNK - 1 :]
                fall = fall_w * (t[c, below, rows, :] - here)
                new = here + (pltpu.roll(east, 1, 1) - east) + (south - north) + (fall - fall_in[c, rows, :])
                new = jnp.where(wet, new, 0.0)
                fall_in[c, rows, :] = fall
                o[c, k, rows, :] = new
                news.append(new)
            fld[0, rows, :] += tk * (news[0] - 0.5 * news[1])
        return 0

    lax.fori_loop(0, nlev, level, 0, unroll=UNROLL)

    k_sub = lax.broadcasted_iota(jnp.int32, (24, nx), 0)
    k_lane = lax.rem(lane, 32)
    side_sub = jnp.zeros((24, nx), f32)
    thick_sub = jnp.zeros((24, nx), f32)
    side_lane = jnp.zeros((8, LANES), f32)
    thick_lane = jnp.zeros((8, LANES), f32)
    for k in range(nlev):
        side_sub = jnp.where(k_sub == k, side[k], side_sub)
        thick_sub = jnp.where(k_sub == k, thick[k], thick_sub)
        side_lane = jnp.where(k_lane[:8] == k, side[k], side_lane)
        thick_lane = jnp.where(lane[:8] == k, thick[k], thick_lane)
        thick_lane = jnp.where(lane[:8] == 32 + k, -0.5 * thick[k], thick_lane)
    side_lane, thick_lane = (jnp.concatenate([x] * (ny // 8), axis=0) for x in (side_lane, thick_lane))

    for copy in edge:
        copy.wait_recv()

    def row_flux(lower, upper, ok):
        lowest = jnp.minimum(lower[72:73, :], upper[72:73, :]) * ok
        is_open = k_sub.astype(f32) < lowest
        half = 0.5 * lower[48:72, :]
        p, q = jnp.where(is_open, half + side_sub, 0.0), jnp.where(is_open, half - side_sub, 0.0)
        out = []
        for c in range(2):
            flux = p * lower[24 * c : 24 * c + 24, :] + q * upper[24 * c : 24 * c + 24, :]
            out.append(jnp.where(is_open, flux, 0.0))
        return out

    def col_flux(came, beyond):
        half = 0.5 * jnp.where(lane < 32, pltpu.roll(came, 64, 1), pltpu.roll(came, 96, 1))
        lowest = jnp.minimum(came[:, 96:97], beyond[:, 96:97])
        flux = (half + side_lane) * came + (half - side_lane) * beyond
        return jnp.where(k_lane.astype(f32) < lowest, flux, 0.0)

    flux_dn = row_flux(got_dn, row_dn, dn_ok)
    flux_up = row_flux(row_up, got_up, up_ok)
    flux_lf = col_flux(got_lf[...], col_lf[...])
    flux_rt = col_flux(col_rt[...], got_rt[...])

    def weighed(flux):
        return jnp.sum(thick_sub * (flux[0] - 0.5 * flux[1]), axis=0, keepdims=True)

    fld[0, 0:1, :] += weighed(flux_dn)
    fld[0, ny - 1 : ny, :] -= weighed(flux_up)
    fld[0, :, :LANES] += jnp.where(lane == 0, jnp.sum(thick_lane * flux_lf, axis=1, keepdims=True), 0.0)
    fld[0, :, nx - LANES :] -= jnp.where(lane == LANES - 1, jnp.sum(thick_lane * flux_rt, axis=1, keepdims=True), 0.0)
    rim_force = rim(0, send_c, recv_c)

    outs = []
    for c, dst in enumerate((o1h, o2h)):
        for k in range(nlev):
            o[c, k, 0:1, :] += flux_dn[c][k : k + 1]
            o[c, k, ny - 1 : ny, :] -= flux_up[c][k : k + 1]
            place = 32 * c + k
            o[c, k, :, :LANES] += jnp.where(lane == 0, pltpu.roll(flux_lf, LANES - place, 1) if place else flux_lf, 0.0)
            o[c, k, :, nx - LANES :] -= jnp.where(lane == LANES - 1, pltpu.roll(flux_rt, LANES - 1 - place, 1), 0.0)
        outs.append(pltpu.make_async_copy(o.at[c], dst, out_sem.at[c]))
        outs[c].start()

    sub8 = lax.broadcasted_iota(jnp.int32, (8, nx), 0) < 4
    sub8c = sub8[:, :LANES]
    lane8 = lax.broadcasted_iota(jnp.int32, (8, LANES), 1) < 64
    lane64 = lane < 64
    row = lax.broadcasted_iota(jnp.int32, (ny + 8, nx + LANES), 0)
    mask = jnp.where(row < ny, 1.0, jnp.where(row < ny + 4, up_ok, dn_ok)).astype(f32)

    def widened(n):
        beside = jnp.where(lane64, h_rt[n], h_lf[n])
        ends = jnp.where(sub8, h_up[n], h_dn[n])
        corner = jnp.where(
            sub8c, jnp.where(lane8, h_cn[3, n], h_cn[2, n]), jnp.where(lane8, h_cn[1, n], h_cn[0, n])
        )
        top = jnp.concatenate([fld[n], beside], axis=1)
        bottom = jnp.concatenate([ends, corner], axis=1)
        return jnp.concatenate([top, bottom], axis=0) * mask

    for copy in rim_fixed:
        copy.wait_recv()
    depth, diag = widened(1), widened(2)
    for copy in rim_force:
        copy.wait_recv()
    tall, wide = ny + 8, nx + LANES

    def operate(a):
        b = pltpu.roll(a, wide - 1, 1)
        cc = pltpu.roll(a, tall - 1, 0)
        d = pltpu.roll(b, tall - 1, 0)
        p = depth * (d - a)
        q = depth * (b - cc)
        return (diag * a - p + pltpu.roll(q, 1, 1) + pltpu.roll(pltpu.roll(p, 1, 1) - q, 1, 0)) * mask

    def moment(a, b):
        prod = a[:ny, :nx] * b[:ny, :nx]
        prod = jnp.sum(prod.reshape(ny // 8, 8, nx), axis=0)
        prod = sum(prod[:, n : n + LANES] for n in range(0, nx, LANES))
        return jnp.sum(prod, axis=0, keepdims=True)

    w0 = widened(0)
    w1 = operate(w0)
    w2 = operate(w1)
    w3 = operate(w2)
    v1r[...] = w1[:ny, :nx]
    v2r[...] = w2[:ny, :nx]
    pairs = ((w0, w0), (w0, w1), (w1, w1), (w1, w2), (w2, w2), (w2, w3))
    mom[...] = jnp.concatenate([moment(a, b) for a, b in pairs] + [jnp.zeros((2, LANES), f32)], axis=0)

    for dy, dx in others:
        send(mom, gath.at[me], gsend, grecv, neighbour(dy, dx))
    gath[me] = mom[...]
    for copy in edge + rim_fixed + rim_force:
        copy.wait_send()
    for copy in outs:
        copy.wait()
    every = gath.at[pl.ds(0, total - 1)]
    pltpu.make_async_copy(every, every, grecv).wait()
    sums = jnp.sum(jnp.sum(gath[...], axis=0), axis=1, keepdims=True)
    moments = [jnp.broadcast_to(sums[n : n + 1], (8, LANES)) for n in range(6)]
    weights = [jnp.concatenate([x] * (nx // LANES), axis=1) for x in iterate_weights(moments)]
    for r in range(0, ny, 8):
        rows = slice(r, r + 8)
        surf[rows, :] = weights[0] * fld[0, rows, :] + weights[1] * v1r[rows, :] + weights[2] * v2r[rows, :]
    pltpu.make_async_copy(every, every, gsend).wait()


def on_device(nby, nbx, t1, t2, u, v, lev, side, vert, thick, cd, dg):
    nlev, ny, nx = t1.shape
    anywhere = pl.BlockSpec(memory_space=pl.ANY)
    vmem = pltpu.VMEM
    dma = pltpu.SemaphoreType.DMA
    cells = nlev * ny * nx
    return pl.pallas_call(
        functools.partial(kernel, nby, nbx, nlev),
        out_shape=(
            jax.ShapeDtypeStruct(t1.shape, f32),
            jax.ShapeDtypeStruct(t1.shape, f32),
            jax.ShapeDtypeStruct((ny, nx), f32),
        ),
        in_specs=[anywhere] * 10,
        out_specs=(anywhere, anywhere, pl.BlockSpec(memory_space=vmem)),
        scratch_shapes=[pltpu.SMEM((nlev,), f32)] * 3
        + [
            vmem((2, nlev, ny, nx), f32),
            vmem((nlev, ny, nx), u.dtype),
            vmem((nlev, ny, nx), v.dtype),
            vmem((ny, nx), jnp.int32),
            vmem((2, nlev, ny, nx), f32),
            vmem((80, nx), f32),
            vmem((80, nx), f32),
            vmem((80, nx), f32),
            vmem((80, nx), f32),
            vmem((ny, LANES), f32),
            vmem((ny, LANES), f32),
            vmem((ny, LANES), f32),
            vmem((ny, LANES), f32),
            vmem((3, ny, nx), f32),
            vmem((2, ny, nx), f32),
            vmem((3, ny, nx), f32),
            vmem((3, 8, nx), f32),
            vmem((3, 8, nx), f32),
            vmem((3, ny, LANES), f32),
            vmem((3, ny, LANES), f32),
            vmem((4, 3, 8, LANES), f32),
            vmem((ny, nx), f32),
            vmem((ny, nx), f32),
            vmem((8, LANES), f32),
            vmem((nby * nbx, 8, LANES), f32),
            dma((10,)),
            dma((2,)),
            dma((4,)),
            dma((4,)),
            dma((8,)),
            dma((8,)),
            dma((8,)),
            dma((8,)),
            dma,
            dma,
        ],
        compiler_params=pltpu.CompilerParams(
            collective_id=0, has_side_effects=True, vmem_limit_bytes=VMEM_MIB * 2**20
        ),
        cost_estimate=pl.CostEstimate(flops=60 * cells, bytes_accessed=20 * cells, transcendentals=0),
    )(side, vert, thick, t1, t2, u, v, lev, cd, dg)


def solution(mesh):
    def body(t1, t2, u, v, lev, side, vert, thick, cd, dg):
        return on_device(mesh.shape["by"], mesh.shape["bx"], t1, t2, u, v, lev, side, vert, thick, cd, dg)

    block, plane = P(None, "by", "bx"), P("by", "bx")
    return jax.shard_map(
        body,
        mesh=mesh,
        in_specs=(block, block, block, block, plane, P(), P(), P(), plane, plane),
        out_specs=(block, block, plane),
        check_vma=False,
    )
```

```python
import functools

import jax
import jax.numpy as jnp
from jax import lax
from jax.experimental import pallas as pl
from jax.experimental.pallas import tpu as pltpu
from jax.sharding import PartitionSpec as P

ITERS = 3
SHIFT = 3.0
CHUNK = 16
PARTS = 3
UNROLL = 2
EARLY = 6
SPLIT = 8
VMEM_MIB = 62
LANES = 128
MESH = pl.DeviceIdType.MESH
f32 = jnp.float32
SIDES = ((1, 0), (-1, 0), (0, 1), (0, -1), (1, 1), (1, -1), (-1, 1), (-1, -1))


def iterate_weights(moments):
    def add(a, b, scale):
        longer = max(len(a), len(b))
        out = []
        for n in range(longer):
            if n >= len(a):
                out.append(scale * b[n])
            elif n >= len(b):
                out.append(a[n])
            else:
                out.append(a[n] + scale * b[n])
        return out

    def operate(a):
        shifted = [SHIFT * x for x in a] + [None]
        for n, x in enumerate(a):
            shifted[n + 1] = x if shifted[n + 1] is None else shifted[n + 1] + x
        return shifted

    def dot(a, b):
        total = None
        for i, x in enumerate(a):
            for j, y in enumerate(b):
                term = x * y * moments[i + j]
                total = term if total is None else total + term
        return total

    residual = [jnp.ones_like(moments[0])]
    image = operate(residual)
    now = dot(residual, residual)
    alpha = now / dot(residual, image)
    direction, along = residual, image
    surface = [jnp.zeros_like(moments[0])]
    for step in range(ITERS):
        surface = add(surface, direction, alpha)
        if step + 1 < ITERS:
            residual = add(residual, along, -alpha)
            image = operate(residual)
            new = dot(residual, residual)
            product = dot(residual, image)
            ratio = new / now
            alpha = new / (product - ratio * new / alpha)
            direction = add(residual, direction, ratio)
            along = add(image, along, ratio)
            now = new
    return surface


def kernel(
    nby, nbx, nlev,
    sideh, verth, thickh, t1h, t2h, uh, vh, levh, cdh, dgh,
    o1h, o2h, surf,
    side, vert, thick, t, u, v, levi, o, row_up, row_dn, got_dn, got_up, col_rt, col_lf, got_lf, got_rt,
    lv, sums, fall_in, fld, h_up, h_dn, h_rt, h_lf, h_cn, v1r, v2r, mom, gath,
    load_sem, out_sem, send_a, recv_a, send_b, recv_b, send_c, recv_c, gsend, grecv,
):
    by, bx = lax.axis_index("by"), lax.axis_index("bx")
    total = nby * nbx
    me = by * nbx + bx
    ny, nx = fld.shape[1], fld.shape[2]

    loads = [
        pltpu.make_async_copy(sideh, side, load_sem.at[8]),
        pltpu.make_async_copy(verth, vert, load_sem.at[9]),
        pltpu.make_async_copy(thickh, thick, load_sem.at[10]),
        pltpu.make_async_copy(levh, levi, load_sem.at[11]),
    ]
    groups = ((0, EARLY), (EARLY, nlev))
    bulk = []
    for g, (first, end) in enumerate(groups):
        span = pl.ds(first, end - first)
        bulk.append([
            pltpu.make_async_copy(t1h.at[span], t.at[0, span], load_sem.at[4 * g]),
            pltpu.make_async_copy(t2h.at[span], t.at[1, span], load_sem.at[4 * g + 1]),
            pltpu.make_async_copy(uh.at[span], u.at[span], load_sem.at[4 * g + 2]),
            pltpu.make_async_copy(vh.at[span], v.at[span], load_sem.at[4 * g + 3]),
        ])
    planes = [
        pltpu.make_async_copy(cdh, fld.at[1], load_sem.at[12]),
        pltpu.make_async_copy(dgh, fld.at[2], load_sem.at[13]),
    ]
    for copy in loads + bulk[0] + bulk[1] + planes:
        copy.start()

    def neighbour(dy, dx):
        y, x = by + dy % nby, bx + dx % nbx
        return (jnp.where(y >= nby, y - nby, y), jnp.where(x >= nbx, x - nbx, x))

    others = [(dy, dx) for dy in range(nby) for dx in range(nbx)][1:]
    barrier = pltpu.get_barrier_semaphore()
    for dy, dx in others:
        pl.semaphore_signal(barrier, inc=1, device_id=neighbour(dy, dx), device_id_type=MESH)

    up_ok = jnp.where(by < nby - 1, 1.0, 0.0).astype(f32)
    dn_ok = jnp.where(by > 0, 1.0, 0.0).astype(f32)

    for copy in loads:
        copy.wait()
    levels = levi[...]
    levf = levels.astype(f32)

    sub_c = lax.broadcasted_iota(jnp.int32, (CHUNK, nx), 0)
    lane_c = lax.broadcasted_iota(jnp.int32, (CHUNK, nx), 1)
    for r in range(0, ny, CHUNK):
        rows = slice(r, r + CHUNK)
        lev = levf[rows]
        lev_rt = jnp.where(lane_c == nx - 1, 0.0, pltpu.roll(lev, nx - 1, 1))
        above = levf[r + CHUNK : r + CHUNK + 1] if r + CHUNK < ny else 0.0
        lev_up = jnp.where(sub_c == CHUNK - 1, above, pltpu.roll(lev, CHUNK - 1, 0))
        lv[0, rows, :] = lev
        lv[1, rows, :] = jnp.minimum(lev, lev_rt)
        lv[2, rows, :] = jnp.minimum(lev, lev_up)
    def force_pass(g):
        start, end = groups[g]

        def rows_of(n, _):
            r = pl.multiple_of(n * CHUNK, CHUNK)
            rows = pl.ds(r, CHUNK)
            above = jnp.minimum(r + CHUNK, ny - 1)
            lev, lev_e, lev_n = lv[0, rows, :], lv[1, rows, :], lv[2, rows, :]
            before = None
            if start:
                before = t[0, start - 1, rows, :] - 0.5 * t[1, start - 1, rows, :]
                acc = [sums[m, rows, :] for m in range(3)]
            else:
                acc = [jnp.zeros((CHUNK, nx), f32)] * 3
            for k in range(start, end):
                g_here = t[0, k, rows, :] - 0.5 * t[1, k, rows, :]
                top = t[0, k, pl.ds(above, 1), :] - 0.5 * t[1, k, pl.ds(above, 1), :]
                g_up = jnp.where(sub_c == CHUNK - 1, top, pltpu.roll(g_here, CHUNK - 1, 0))
                g_rt = pltpu.roll(g_here, nx - 1, 1)
                twice = 2.0 * side[k]
                east = u[k, rows, :].astype(f32) * (g_here + g_rt) - twice * (g_rt - g_here)
                north = v[k, rows, :].astype(f32) * (g_here + g_up) - twice * (g_up - g_here)
                inside = thick[k] * g_here
                if k:
                    inside = inside + (vert[k - 1] * (thick[k - 1] - thick[k])) * (g_here - before)
                half = 0.5 * thick[k]
                acc[0] = acc[0] + jnp.where(lev > k, inside, 0.0)
                acc[1] = acc[1] + half * jnp.where(lev_e > k, east, 0.0)
                acc[2] = acc[2] + half * jnp.where(lev_n > k, north, 0.0)
                before = g_here
            for m in range(3):
                sums[m, rows, :] = acc[m]
            return 0

        lax.fori_loop(0, ny // CHUNK, rows_of, 0)

    for copy in bulk[0]:
        copy.wait()
    force_pass(0)
    for copy in bulk[1]:
        copy.wait()

    lane = lax.broadcasted_iota(jnp.int32, (ny, LANES), 1)
    row_up[pl.ds(72, 8), :] = jnp.broadcast_to(levf[ny - 1 : ny], (8, nx))
    row_dn[pl.ds(72, 8), :] = jnp.broadcast_to(levf[0:1], (8, nx))
    right = jnp.where(lane == 96, pltpu.roll(levf[:, nx - LANES :], 97, 1), 0.0)
    left = jnp.where(lane == 96, pltpu.roll(levf[:, :LANES], 96, 1), 0.0)
    for c in range(2):
        for k in range(nlev):
            row_up[24 * c + k : 24 * c + k + 1, :] = t[c, k, ny - 1 : ny, :]
            row_dn[24 * c + k : 24 * c + k + 1, :] = t[c, k, 0:1, :]
            place = 32 * c + k
            right = jnp.where(lane == place, pltpu.roll(t[c, k, :, nx - LANES :], place + 1, 1), right)
            tile = t[c, k, :, :LANES]
            left = jnp.where(lane == place, pltpu.roll(tile, place, 1) if place else tile, left)
    for k in range(nlev):
        right = jnp.where(lane == 64 + k, pltpu.roll(u[k, :, nx - LANES :].astype(f32), 65 + k, 1), right)
    for k in range(nlev):
        row_up[48 + k : 49 + k, :] = v[k, ny - 16 :, :].astype(f32)[15:16]
    col_rt[...] = right
    col_lf[...] = left

    pl.semaphore_wait(barrier, total - 1)

    def send(src, dst, ssem, rsem, to):
        copy = pltpu.make_async_remote_copy(
            src_ref=src, dst_ref=dst, send_sem=ssem, recv_sem=rsem, device_id=to, device_id_type=MESH
        )
        copy.start()
        return copy

    edge = [
        send(row_up, got_dn, send_a.at[0], recv_a.at[0], neighbour(1, 0)),
        send(row_dn, got_up, send_a.at[1], recv_a.at[1], neighbour(-1, 0)),
        send(col_rt, got_lf, send_a.at[2], recv_a.at[2], neighbour(0, 1)),
        send(col_lf, got_rt, send_a.at[3], recv_a.at[3], neighbour(0, -1)),
    ]

    def rim(which, ssem, rsem):
        copies = []
        for n, (dy, dx) in enumerate(SIDES):
            rows = pl.ds(0, ny) if dy == 0 else (pl.ds(ny - 8, 8) if dy > 0 else pl.ds(0, 8))
            cols = pl.ds(0, nx) if dx == 0 else (pl.ds(nx - LANES, LANES) if dx > 0 else pl.ds(0, LANES))
            place = {0: h_dn, 1: h_up, 2: h_lf, 3: h_rt}.get(n)
            dst = h_cn.at[n - 4, which] if place is None else place.at[which]
            copies.append(send(fld.at[which, rows, cols], dst, ssem.at[n], rsem.at[n], neighbour(dy, dx)))
        return copies

    for copy in planes:
        copy.wait()
    fld[1] = fld[1] * jnp.where(levels > 0, 0.5, 0.0).astype(f32)
    fld[2] = fld[2] - SHIFT
    rim_fixed = rim(pl.ds(1, 2), send_b, recv_b)

    force_pass(1)
    force = sums[0] + (pltpu.roll(sums[1], 1, 1) - sums[1]) + (pltpu.roll(sums[2], 1, 0) - sums[2])
    fld[0] = force

    def level(k, _):
        kf = k.astype(f32)
        s, vk = side[k], vert[k]
        below = jnp.minimum(k + 1, nlev - 1)
        last = [0.0, 0.0]
        for r in range(0, ny, CHUNK):
            rows = slice(r, r + CHUNK)
            lev = lv[0, rows, :]
            hu = 0.5 * u[k, rows, :].astype(f32)
            hv = 0.5 * v[k, rows, :].astype(f32)
            in_e, in_n = kf < lv[1, rows, :], kf < lv[2, rows, :]
            pe, qe = jnp.where(in_e, hu + s, 0.0), jnp.where(in_e, hu - s, 0.0)
            pn, qn = jnp.where(in_n, hv + s, 0.0), jnp.where(in_n, hv - s, 0.0)
            wet = kf < lev
            fall_w = jnp.where(kf + 1.0 < lev, vk, 0.0)
            for c in range(2):
                here = t[c, k, rows, :]
                upper = pltpu.roll(here, CHUNK - 1, 0)
                if r + CHUNK < ny:
                    upper = jnp.where(sub_c == CHUNK - 1, t[c, k, r + CHUNK : r + CHUNK + 1, :], upper)
                east = pe * here + qe * pltpu.roll(here, nx - 1, 1)
                north = pn * here + qn * upper
                south = jnp.where(sub_c == 0, last[c], pltpu.roll(north, 1, 0))
                last[c] = north[CHUNK - 1 :]
                fall = fall_w * (t[c, below, rows, :] - here)
                new = here + (pltpu.roll(east, 1, 1) - east) + (south - north) + (fall - fall_in[c, rows, :])
                new = jnp.where(wet, new, 0.0)
                fall_in[c, rows, :] = fall
                o[c, k, rows, :] = new
        return 0

    k_sub = lax.broadcasted_iota(jnp.int32, (24, nx), 0)
    k_lane = lax.rem(lane, 32)
    side_sub = jnp.zeros((24, nx), f32)
    thick_sub = jnp.zeros((24, nx), f32)
    side_lane = jnp.zeros((8, LANES), f32)
    thick_lane = jnp.zeros((8, LANES), f32)
    for k in range(nlev):
        side_sub = jnp.where(k_sub == k, side[k], side_sub)
        thick_sub = jnp.where(k_sub == k, thick[k], thick_sub)
        side_lane = jnp.where(k_lane[:8] == k, side[k], side_lane)
        thick_lane = jnp.where(lane[:8] == k, thick[k], thick_lane)
        thick_lane = jnp.where(lane[:8] == 32 + k, -0.5 * thick[k], thick_lane)
    side_lane, thick_lane = (jnp.concatenate([x] * (ny // 8), axis=0) for x in (side_lane, thick_lane))

    for copy in edge:
        copy.wait_recv()

    def row_flux(lower, upper, ok):
        lowest = jnp.minimum(lower[72:73, :], upper[72:73, :]) * ok
        is_open = k_sub.astype(f32) < lowest
        half = 0.5 * lower[48:72, :]
        p, q = jnp.where(is_open, half + side_sub, 0.0), jnp.where(is_open, half - side_sub, 0.0)
        out = []
        for c in range(2):
            flux = p * lower[24 * c : 24 * c + 24, :] + q * upper[24 * c : 24 * c + 24, :]
            out.append(jnp.where(is_open, flux, 0.0))
        return out

    def col_flux(came, beyond):
        half = 0.5 * jnp.where(lane < 32, pltpu.roll(came, 64, 1), pltpu.roll(came, 96, 1))
        lowest = jnp.minimum(came[:, 96:97], beyond[:, 96:97])
        flux = (half + side_lane) * came + (half - side_lane) * beyond
        return jnp.where(k_lane.astype(f32) < lowest, flux, 0.0)

    flux_dn = row_flux(got_dn, row_dn, dn_ok)
    flux_up = row_flux(row_up, got_up, up_ok)
    flux_lf = col_flux(got_lf[...], col_lf[...])
    flux_rt = col_flux(col_rt[...], got_rt[...])

    def weighed(flux):
        return jnp.sum(thick_sub * (flux[0] - 0.5 * flux[1]), axis=0, keepdims=True)

    fld[0, 0:1, :] += weighed(flux_dn)
    fld[0, ny - 1 : ny, :] -= weighed(flux_up)
    fld[0, :, :LANES] += jnp.where(lane == 0, jnp.sum(thick_lane * flux_lf, axis=1, keepdims=True), 0.0)
    fld[0, :, nx - LANES :] -= jnp.where(lane == LANES - 1, jnp.sum(thick_lane * flux_rt, axis=1, keepdims=True), 0.0)
    rim_force = rim(0, send_c, recv_c)

    outs = []

    def tracer_pass(first, end):
        lax.fori_loop(first, end, level, 0, unroll=UNROLL)
        for c, dst in enumerate((o1h, o2h)):
            for k in range(first, end):
                o[c, k, 0:1, :] += flux_dn[c][k : k + 1]
                o[c, k, ny - 1 : ny, :] -= flux_up[c][k : k + 1]
                place = 32 * c + k
                o[c, k, :, :LANES] += jnp.where(lane == 0, pltpu.roll(flux_lf, LANES - place, 1) if place else flux_lf, 0.0)
                o[c, k, :, nx - LANES :] -= jnp.where(lane == LANES - 1, pltpu.roll(flux_rt, LANES - 1 - place, 1), 0.0)
            span = pl.ds(first, end - first)
            copy = pltpu.make_async_copy(o.at[c, span], dst.at[span], out_sem.at[len(outs)])
            copy.start()
            outs.append(copy)

    fall_in[...] = jnp.zeros_like(fall_in)
    tracer_pass(0, SPLIT)

    sub8 = lax.broadcasted_iota(jnp.int32, (8, nx), 0) < 4
    sub8c = sub8[:, :LANES]
    lane8 = lax.broadcasted_iota(jnp.int32, (8, LANES), 1) < 64
    lane64 = lane < 64
    row = lax.broadcasted_iota(jnp.int32, (ny + 8, nx + LANES), 0)
    mask = jnp.where(row < ny, 1.0, jnp.where(row < ny + 4, up_ok, dn_ok)).astype(f32)

    def widened(n):
        beside = jnp.where(lane64, h_rt[n], h_lf[n])
        ends = jnp.where(sub8, h_up[n], h_dn[n])
        corner = jnp.where(
            sub8c, jnp.where(lane8, h_cn[3, n], h_cn[2, n]), jnp.where(lane8, h_cn[1, n], h_cn[0, n])
        )
        top = jnp.concatenate([fld[n], beside], axis=1)
        bottom = jnp.concatenate([ends, corner], axis=1)
        return jnp.concatenate([top, bottom], axis=0) * mask

    for copy in rim_fixed:
        copy.wait_recv()
    depth, diag = widened(1), widened(2)
    for copy in rim_force:
        copy.wait_recv()
    tall, wide = ny + 8, nx + LANES

    def operate(a):
        b = pltpu.roll(a, wide - 1, 1)
        cc = pltpu.roll(a, tall - 1, 0)
        d = pltpu.roll(b, tall - 1, 0)
        p = depth * (d - a)
        q = depth * (b - cc)
        return (diag * a - p + pltpu.roll(q, 1, 1) + pltpu.roll(pltpu.roll(p, 1, 1) - q, 1, 0)) * mask

    def moment(a, b):
        prod = a[:ny, :nx] * b[:ny, :nx]
        prod = jnp.sum(prod.reshape(ny // 8, 8, nx), axis=0)
        prod = sum(prod[:, n : n + LANES] for n in range(0, nx, LANES))
        return jnp.sum(prod, axis=0, keepdims=True)

    w0 = widened(0)
    w1 = operate(w0)
    w2 = operate(w1)
    w3 = operate(w2)
    v1r[...] = w1[:ny, :nx]
    v2r[...] = w2[:ny, :nx]
    pairs = ((w0, w0), (w0, w1), (w1, w1), (w1, w2), (w2, w2), (w2, w3))
    mom[...] = jnp.concatenate([moment(a, b) for a, b in pairs] + [jnp.zeros((2, LANES), f32)], axis=0)

    for dy, dx in others:
        send(mom, gath.at[me], gsend, grecv, neighbour(dy, dx))
    gath[me] = mom[...]
    tracer_pass(SPLIT, nlev)
    for copy in edge + rim_fixed + rim_force:
        copy.wait_send()
    for copy in outs:
        copy.wait()
    every = gath.at[pl.ds(0, total - 1)]
    pltpu.make_async_copy(every, every, grecv).wait()
    whole = jnp.sum(jnp.sum(gath[...], axis=0), axis=1, keepdims=True)
    moments = [jnp.broadcast_to(whole[n : n + 1], (8, LANES)) for n in range(6)]
    weights = [jnp.concatenate([x] * (nx // LANES), axis=1) for x in iterate_weights(moments)]
    for r in range(0, ny, 8):
        rows = slice(r, r + 8)
        surf[rows, :] = weights[0] * fld[0, rows, :] + weights[1] * v1r[rows, :] + weights[2] * v2r[rows, :]
    pltpu.make_async_copy(every, every, gsend).wait()


def on_device(nby, nbx, t1, t2, u, v, lev, side, vert, thick, cd, dg):
    nlev, ny, nx = t1.shape
    anywhere = pl.BlockSpec(memory_space=pl.ANY)
    vmem = pltpu.VMEM
    dma = pltpu.SemaphoreType.DMA
    cells = nlev * ny * nx
    made = pl.pallas_call(
        functools.partial(kernel, nby, nbx, nlev),
        out_shape=(
            jax.ShapeDtypeStruct(t1.shape, f32),
            jax.ShapeDtypeStruct(t1.shape, f32),
            jax.ShapeDtypeStruct((ny, nx), f32),
        ),
        in_specs=[anywhere] * 10,
        out_specs=(anywhere, anywhere, pl.BlockSpec(memory_space=vmem)),
        scratch_shapes=[pltpu.SMEM((nlev,), f32)] * 3
        + [
            vmem((2, nlev, ny, nx), f32),
            vmem((nlev, ny, nx), u.dtype),
            vmem((nlev, ny, nx), v.dtype),
            vmem((ny, nx), jnp.int32),
            vmem((2, nlev, ny, nx), f32),
            vmem((80, nx), f32),
            vmem((80, nx), f32),
            vmem((80, nx), f32),
            vmem((80, nx), f32),
            vmem((ny, LANES), f32),
            vmem((ny, LANES), f32),
            vmem((ny, LANES), f32),
            vmem((ny, LANES), f32),
            vmem((3, ny, nx), f32),
            vmem((3, ny, nx), f32),
            vmem((2, ny, nx), f32),
            vmem((3, ny, nx), f32),
            vmem((3, 8, nx), f32),
            vmem((3, 8, nx), f32),
            vmem((3, ny, LANES), f32),
            vmem((3, ny, LANES), f32),
            vmem((4, 3, 8, LANES), f32),
            vmem((ny, nx), f32),
            vmem((ny, nx), f32),
            vmem((8, LANES), f32),
            vmem((nby * nbx, 8, LANES), f32),
            dma((14,)),
            dma((4,)),
            dma((4,)),
            dma((4,)),
            dma((8,)),
            dma((8,)),
            dma((8,)),
            dma((8,)),
            dma,
            dma,
        ],
        compiler_params=pltpu.CompilerParams(
            collective_id=0, has_side_effects=True, vmem_limit_bytes=VMEM_MIB * 2**20
        ),
        cost_estimate=pl.CostEstimate(flops=60 * cells, bytes_accessed=20 * cells, transcendentals=0),
    )(side, vert, thick, t1, t2, u, v, lev, cd, dg)

    return pl.pallas_call(
        hand_on,
        out_shape=tuple(jax.ShapeDtypeStruct(x.shape, x.dtype) for x in made),
        in_specs=[anywhere] * 3,
        out_specs=(anywhere,) * 3,
        scratch_shapes=[dma((2 * PARTS + 1,))],
        compiler_params=pltpu.CompilerParams(vmem_limit_bytes=VMEM_MIB * 2**20),
        cost_estimate=pl.CostEstimate(flops=0, bytes_accessed=16 * cells, transcendentals=0),
    )(*made)


def hand_on(a, b, c, a_out, b_out, c_out, sems):
    copies = [pltpu.make_async_copy(c, c_out, sems.at[2 * PARTS])]
    step = a.shape[0] // PARTS
    for n in range(PARTS):
        span = pl.ds(n * step, step)
        copies.append(pltpu.make_async_copy(a.at[span], a_out.at[span], sems.at[2 * n]))
        copies.append(pltpu.make_async_copy(b.at[span], b_out.at[span], sems.at[2 * n + 1]))
    for copy in copies:
        copy.start()
    for copy in copies:
        copy.wait()


def solution(mesh):
    def body(t1, t2, u, v, lev, side, vert, thick, cd, dg):
        return on_device(mesh.shape["by"], mesh.shape["bx"], t1, t2, u, v, lev, side, vert, thick, cd, dg)

    block, plane = P(None, "by", "bx"), P("by", "bx")
    return jax.shard_map(
        body,
        mesh=mesh,
        in_specs=(block, block, block, block, plane, P(), P(), P(), plane, plane),
        out_specs=(block, block, plane),
        check_vma=False,
    )
```

```python
import functools

import jax
import jax.numpy as jnp
from jax import lax
from jax.experimental import pallas as pl
from jax.experimental.pallas import tpu as pltpu
from jax.sharding import PartitionSpec as P

ITERS = 3
SHIFT = 3.0
CHUNK = 16
PARTS = 3
EARLY = 6
SPLIT = 8
VMEM_MIB = 62
LANES = 128
MESH = pl.DeviceIdType.MESH
f32 = jnp.float32
SIDES = ((1, 0), (-1, 0), (0, 1), (0, -1), (1, 1), (1, -1), (-1, 1), (-1, -1))


def iterate_weights(moments):
    def add(a, b, scale):
        longer = max(len(a), len(b))
        out = []
        for n in range(longer):
            if n >= len(a):
                out.append(scale * b[n])
            elif n >= len(b):
                out.append(a[n])
            else:
                out.append(a[n] + scale * b[n])
        return out

    def operate(a):
        shifted = [SHIFT * x for x in a] + [None]
        for n, x in enumerate(a):
            shifted[n + 1] = x if shifted[n + 1] is None else shifted[n + 1] + x
        return shifted

    def dot(a, b):
        total = None
        for i, x in enumerate(a):
            for j, y in enumerate(b):
                term = x * y * moments[i + j]
                total = term if total is None else total + term
        return total

    residual = [jnp.ones_like(moments[0])]
    image = operate(residual)
    now = dot(residual, residual)
    alpha = now / dot(residual, image)
    direction, along = residual, image
    surface = [jnp.zeros_like(moments[0])]
    for step in range(ITERS):
        surface = add(surface, direction, alpha)
        if step + 1 < ITERS:
            residual = add(residual, along, -alpha)
            image = operate(residual)
            new = dot(residual, residual)
            product = dot(residual, image)
            ratio = new / now
            alpha = new / (product - ratio * new / alpha)
            direction = add(residual, direction, ratio)
            along = add(image, along, ratio)
            now = new
    return surface


def kernel(
    nby, nbx, nlev,
    sideh, verth, thickh, t1h, t2h, uh, vh, levh, cdh, dgh,
    o1h, o2h, surf,
    side, vert, thick, t, u, v, levi, o, row_up, row_dn, got_dn, got_up, col_rt, col_lf, got_lf, got_rt,
    lv, sums, fall_in, flx, rows_up, cols, fld, h_up, h_dn, h_rt, h_lf, h_cn, v1r, v2r, mom, gath,
    load_sem, out_sem, send_a, recv_a, send_b, recv_b, send_c, recv_c, gsend, grecv,
):
    by, bx = lax.axis_index("by"), lax.axis_index("bx")
    total = nby * nbx
    me = by * nbx + bx
    ny, nx = fld.shape[1], fld.shape[2]

    loads = [
        pltpu.make_async_copy(sideh, side, load_sem.at[8]),
        pltpu.make_async_copy(verth, vert, load_sem.at[9]),
        pltpu.make_async_copy(thickh, thick, load_sem.at[10]),
        pltpu.make_async_copy(levh, levi, load_sem.at[11]),
    ]
    groups = ((0, EARLY), (EARLY, nlev))
    bulk = []
    for g, (first, end) in enumerate(groups):
        span = pl.ds(first, end - first)
        bulk.append([
            pltpu.make_async_copy(t1h.at[span], t.at[0, span], load_sem.at[4 * g]),
            pltpu.make_async_copy(t2h.at[span], t.at[1, span], load_sem.at[4 * g + 1]),
            pltpu.make_async_copy(uh.at[span], u.at[span], load_sem.at[4 * g + 2]),
            pltpu.make_async_copy(vh.at[span], v.at[span], load_sem.at[4 * g + 3]),
        ])
    planes = [
        pltpu.make_async_copy(cdh, fld.at[1], load_sem.at[12]),
        pltpu.make_async_copy(dgh, fld.at[2], load_sem.at[13]),
    ]
    for copy in loads + bulk[0] + bulk[1] + planes:
        copy.start()

    def neighbour(dy, dx):
        y, x = by + dy % nby, bx + dx % nbx
        return (jnp.where(y >= nby, y - nby, y), jnp.where(x >= nbx, x - nbx, x))

    others = [(dy, dx) for dy in range(nby) for dx in range(nbx)][1:]
    barrier = pltpu.get_barrier_semaphore()
    for dy, dx in others:
        pl.semaphore_signal(barrier, inc=1, device_id=neighbour(dy, dx), device_id_type=MESH)

    up_ok = jnp.where(by < nby - 1, 1.0, 0.0).astype(f32)
    dn_ok = jnp.where(by > 0, 1.0, 0.0).astype(f32)

    for copy in loads:
        copy.wait()
    levels = levi[...]
    levf = levels.astype(f32)

    sub_c = lax.broadcasted_iota(jnp.int32, (CHUNK, nx), 0)
    lane_c = lax.broadcasted_iota(jnp.int32, (CHUNK, nx), 1)
    for r in range(0, ny, CHUNK):
        rows = slice(r, r + CHUNK)
        lev = levf[rows]
        lev_rt = jnp.where(lane_c == nx - 1, 0.0, pltpu.roll(lev, nx - 1, 1))
        above = levf[r + CHUNK : r + CHUNK + 1] if r + CHUNK < ny else 0.0
        lev_up = jnp.where(sub_c == CHUNK - 1, above, pltpu.roll(lev, CHUNK - 1, 0))
        lv[0, rows, :] = lev
        lv[1, rows, :] = jnp.minimum(lev, lev_rt)
        lv[2, rows, :] = jnp.minimum(lev, lev_up)
    def force_pass(g):
        start, end = groups[g]

        def rows_of(n, _):
            r = pl.multiple_of(n * CHUNK, CHUNK)
            rows = pl.ds(r, CHUNK)
            above = jnp.minimum(r + CHUNK, ny - 1)
            lev, lev_e, lev_n = lv[0, rows, :], lv[1, rows, :], lv[2, rows, :]
            before = None
            if start:
                before = t[0, start - 1, rows, :] - 0.5 * t[1, start - 1, rows, :]
                acc = [sums[m, rows, :] for m in range(3)]
            else:
                acc = [jnp.zeros((CHUNK, nx), f32)] * 3
            for k in range(start, end):
                g_here = t[0, k, rows, :] - 0.5 * t[1, k, rows, :]
                top = t[0, k, pl.ds(above, 1), :] - 0.5 * t[1, k, pl.ds(above, 1), :]
                g_up = jnp.where(sub_c == CHUNK - 1, top, pltpu.roll(g_here, CHUNK - 1, 0))
                g_rt = pltpu.roll(g_here, nx - 1, 1)
                twice = 2.0 * side[k]
                east = u[k, rows, :].astype(f32) * (g_here + g_rt) - twice * (g_rt - g_here)
                north = v[k, rows, :].astype(f32) * (g_here + g_up) - twice * (g_up - g_here)
                inside = thick[k] * g_here
                if k:
                    inside = inside + (vert[k - 1] * (thick[k - 1] - thick[k])) * (g_here - before)
                half = 0.5 * thick[k]
                acc[0] = acc[0] + jnp.where(lev > k, inside, 0.0)
                acc[1] = acc[1] + half * jnp.where(lev_e > k, east, 0.0)
                acc[2] = acc[2] + half * jnp.where(lev_n > k, north, 0.0)
                before = g_here
            for m in range(3):
                sums[m, rows, :] = acc[m]
            return 0

        lax.fori_loop(0, ny // CHUNK, rows_of, 0)

    for copy in bulk[0]:
        copy.wait()
    force_pass(0)
    for copy in bulk[1]:
        copy.wait()

    lane = lax.broadcasted_iota(jnp.int32, (ny, LANES), 1)
    row_up[pl.ds(72, 8), :] = jnp.broadcast_to(levf[ny - 1 : ny], (8, nx))
    row_dn[pl.ds(72, 8), :] = jnp.broadcast_to(levf[0:1], (8, nx))
    right = jnp.where(lane == 96, pltpu.roll(levf[:, nx - LANES :], 97, 1), 0.0)
    left = jnp.where(lane == 96, pltpu.roll(levf[:, :LANES], 96, 1), 0.0)
    for c in range(2):
        for k in range(nlev):
            place = 32 * c + k
            right = jnp.where(lane == place, pltpu.roll(t[c, k, :, nx - LANES :], place + 1, 1), right)
            tile = t[c, k, :, :LANES]
            left = jnp.where(lane == place, pltpu.roll(tile, place, 1) if place else tile, left)
    for k in range(nlev):
        right = jnp.where(lane == 64 + k, pltpu.roll(u[k, :, nx - LANES :].astype(f32), 65 + k, 1), right)
    for c in range(2):
        upper = [t[c, k, ny - 1 : ny, :] for k in range(nlev)]
        lower = [t[c, k, 0:1, :] for k in range(nlev)]
        for k in range(nlev):
            row_up[24 * c + k : 24 * c + k + 1, :] = upper[k]
            row_dn[24 * c + k : 24 * c + k + 1, :] = lower[k]
    upper = [v[k, ny - 16 :, :].astype(f32)[15:16] for k in range(nlev)]
    for k in range(nlev):
        row_up[48 + k : 49 + k, :] = upper[k]
    col_rt[...] = right
    col_lf[...] = left

    pl.semaphore_wait(barrier, total - 1)

    def send(src, dst, ssem, rsem, to):
        copy = pltpu.make_async_remote_copy(
            src_ref=src, dst_ref=dst, send_sem=ssem, recv_sem=rsem, device_id=to, device_id_type=MESH
        )
        copy.start()
        return copy

    edge = [
        send(row_up, got_dn, send_a.at[0], recv_a.at[0], neighbour(1, 0)),
        send(row_dn, got_up, send_a.at[1], recv_a.at[1], neighbour(-1, 0)),
        send(col_rt, got_lf, send_a.at[2], recv_a.at[2], neighbour(0, 1)),
        send(col_lf, got_rt, send_a.at[3], recv_a.at[3], neighbour(0, -1)),
    ]

    def rim(which, ssem, rsem):
        copies = []
        for n, (dy, dx) in enumerate(SIDES):
            rows = pl.ds(0, ny) if dy == 0 else (pl.ds(ny - 8, 8) if dy > 0 else pl.ds(0, 8))
            cols = pl.ds(0, nx) if dx == 0 else (pl.ds(nx - LANES, LANES) if dx > 0 else pl.ds(0, LANES))
            place = {0: h_dn, 1: h_up, 2: h_lf, 3: h_rt}.get(n)
            dst = h_cn.at[n - 4, which] if place is None else place.at[which]
            copies.append(send(fld.at[which, rows, cols], dst, ssem.at[n], rsem.at[n], neighbour(dy, dx)))
        return copies

    for copy in planes:
        copy.wait()
    fld[1] = fld[1] * jnp.where(levels > 0, 0.5, 0.0).astype(f32)
    fld[2] = fld[2] - SHIFT
    rim_fixed = rim(pl.ds(1, 2), send_b, recv_b)

    force_pass(1)
    force = sums[0] + (pltpu.roll(sums[1], 1, 1) - sums[1]) + (pltpu.roll(sums[2], 1, 0) - sums[2])
    fld[0] = force

    k_sub = lax.broadcasted_iota(jnp.int32, (24, nx), 0)
    k_lane = lax.rem(lane, 32)
    side_sub = jnp.zeros((24, nx), f32)
    thick_sub = jnp.zeros((24, nx), f32)
    side_lane = jnp.zeros((8, LANES), f32)
    thick_lane = jnp.zeros((8, LANES), f32)
    for k in range(nlev):
        side_sub = jnp.where(k_sub == k, side[k], side_sub)
        thick_sub = jnp.where(k_sub == k, thick[k], thick_sub)
        side_lane = jnp.where(k_lane[:8] == k, side[k], side_lane)
        thick_lane = jnp.where(lane[:8] == k, thick[k], thick_lane)
        thick_lane = jnp.where(lane[:8] == 32 + k, -0.5 * thick[k], thick_lane)
    side_lane, thick_lane = (jnp.concatenate([x] * (ny // 8), axis=0) for x in (side_lane, thick_lane))

    for copy in edge:
        copy.wait_recv()

    def row_flux(lower, upper, ok):
        lowest = jnp.minimum(lower[72:73, :], upper[72:73, :]) * ok
        is_open = k_sub.astype(f32) < lowest
        half = 0.5 * lower[48:72, :]
        p, q = jnp.where(is_open, half + side_sub, 0.0), jnp.where(is_open, half - side_sub, 0.0)
        out = []
        for c in range(2):
            flux = p * lower[24 * c : 24 * c + 24, :] + q * upper[24 * c : 24 * c + 24, :]
            out.append(jnp.where(is_open, flux, 0.0))
        return out

    def col_flux(came, beyond):
        half = 0.5 * jnp.where(lane < 32, pltpu.roll(came, 64, 1), pltpu.roll(came, 96, 1))
        lowest = jnp.minimum(came[:, 96:97], beyond[:, 96:97])
        flux = (half + side_lane) * came + (half - side_lane) * beyond
        return jnp.where(k_lane.astype(f32) < lowest, flux, 0.0)

    flux_dn = row_flux(got_dn, row_dn, dn_ok)
    flux_up = row_flux(row_up, got_up, up_ok)
    flux_lf = col_flux(got_lf[...], col_lf[...])
    flux_rt = col_flux(col_rt[...], got_rt[...])

    def weighed(flux):
        return jnp.sum(thick_sub * (flux[0] - 0.5 * flux[1]), axis=0, keepdims=True)

    fld[0, 0:1, :] += weighed(flux_dn)
    fld[0, ny - 1 : ny, :] -= weighed(flux_up)
    fld[0, :, :LANES] += jnp.where(lane == 0, jnp.sum(thick_lane * flux_lf, axis=1, keepdims=True), 0.0)
    fld[0, :, nx - LANES :] -= jnp.where(lane == LANES - 1, jnp.sum(thick_lane * flux_rt, axis=1, keepdims=True), 0.0)
    rim_force = rim(0, send_c, recv_c)

    outs = []
    for c in range(2):
        flx[c] = flux_dn[c]
        rows_up[c] = flux_up[c]
    cols[0] = flux_lf
    cols[1] = flux_rt
    fall_in[...] = jnp.zeros_like(fall_in)
    lane_t = lane[:CHUNK]

    def tracer_pass(first, end):
        def rows_of(n, _):
            r = pl.multiple_of(n * CHUNK, CHUNK)
            rows = pl.ds(r, CHUNK)
            above = jnp.minimum(r + CHUNK, ny - 1)
            lev, lev_e, lev_n = lv[0, rows, :], lv[1, rows, :], lv[2, rows, :]
            from_lf, from_rt = cols[0, rows, :], cols[1, rows, :]
            falls = [fall_in[c, rows, :] for c in range(2)]
            pending = []
            for k in range(first, end):
                here = [t[c, k, rows, :] for c in range(2)]
                top = [t[c, k, pl.ds(above, 1), :] for c in range(2)]
                under = [flx[c, k : k + 1, :] for c in range(2)]
                below = [t[c, k + 1, rows, :] for c in range(2)] if k + 1 < nlev else None
                hu = 0.5 * u[k, rows, :].astype(f32)
                hv = 0.5 * v[k, rows, :].astype(f32)
                for ref, where, value in pending:
                    ref[where] = value
                pending = []
                s = side[k]
                in_e, in_n = lev_e > k, lev_n > k
                pe, qe = jnp.where(in_e, hu + s, 0.0), jnp.where(in_e, hu - s, 0.0)
                pn, qn = jnp.where(in_n, hv + s, 0.0), jnp.where(in_n, hv - s, 0.0)
                wet = lev > k
                if k + 1 < nlev:
                    fall_w = jnp.where(lev > k + 1, vert[k], 0.0)
                for c in range(2):
                    x = here[c]
                    up = jnp.where(sub_c == CHUNK - 1, top[c], pltpu.roll(x, CHUNK - 1, 0))
                    east = pe * x + qe * pltpu.roll(x, nx - 1, 1)
                    north = pn * x + qn * up
                    south = jnp.where(sub_c == 0, under[c], pltpu.roll(north, 1, 0))
                    place = 32 * c + k
                    lf = pltpu.roll(from_lf, LANES - place, 1) if place else from_lf
                    rt = pltpu.roll(from_rt, LANES - 1 - place, 1)
                    shared = jnp.concatenate(
                        [jnp.where(lane_t == 0, lf, 0.0)]
                        + [jnp.zeros((CHUNK, LANES), f32)] * (nx // LANES - 2)
                        + [jnp.where(lane_t == LANES - 1, -rt, 0.0)],
                        axis=1,
                    )
                    new = x + (pltpu.roll(east, 1, 1) - east + shared) + (south - north) - falls[c]
                    if k + 1 < nlev:
                        falls[c] = fall_w * (below[c] - x)
                        new = new + falls[c]
                    pending.append((o, (c, k, rows), jnp.where(wet, new, 0.0)))
                    pending.append((flx, (c, slice(k, k + 1)), north[CHUNK - 1 :]))
            for ref, where, value in pending:
                ref[where] = value
            for c in range(2):
                fall_in[c, rows, :] = falls[c]
            return 0

        lax.fori_loop(0, ny // CHUNK, rows_of, 0)
        span = pl.ds(first, end - first)
        for c, dst in enumerate((o1h, o2h)):
            ends = [o[c, k, ny - 1 : ny, :] - rows_up[c, k : k + 1, :] for k in range(first, end)]
            for k in range(first, end):
                o[c, k, ny - 1 : ny, :] = ends[k - first]
            copy = pltpu.make_async_copy(o.at[c, span], dst.at[span], out_sem.at[len(outs)])
            copy.start()
            outs.append(copy)

    tracer_pass(0, SPLIT)

    sub8 = lax.broadcasted_iota(jnp.int32, (8, nx), 0) < 4
    sub8c = sub8[:, :LANES]
    lane8 = lax.broadcasted_iota(jnp.int32, (8, LANES), 1) < 64
    lane64 = lane < 64
    row = lax.broadcasted_iota(jnp.int32, (ny + 8, nx + LANES), 0)
    mask = jnp.where(row < ny, 1.0, jnp.where(row < ny + 4, up_ok, dn_ok)).astype(f32)

    def widened(n):
        beside = jnp.where(lane64, h_rt[n], h_lf[n])
        ends = jnp.where(sub8, h_up[n], h_dn[n])
        corner = jnp.where(
            sub8c, jnp.where(lane8, h_cn[3, n], h_cn[2, n]), jnp.where(lane8, h_cn[1, n], h_cn[0, n])
        )
        top = jnp.concatenate([fld[n], beside], axis=1)
        bottom = jnp.concatenate([ends, corner], axis=1)
        return jnp.concatenate([top, bottom], axis=0) * mask

    for copy in rim_fixed:
        copy.wait_recv()
    depth, diag = widened(1), widened(2)
    for copy in rim_force:
        copy.wait_recv()
    tall, wide = ny + 8, nx + LANES

    def operate(a):
        b = pltpu.roll(a, wide - 1, 1)
        cc = pltpu.roll(a, tall - 1, 0)
        d = pltpu.roll(b, tall - 1, 0)
        p = depth * (d - a)
        q = depth * (b - cc)
        return (diag * a - p + pltpu.roll(q, 1, 1) + pltpu.roll(pltpu.roll(p, 1, 1) - q, 1, 0)) * mask

    def moment(a, b):
        prod = a[:ny, :nx] * b[:ny, :nx]
        prod = jnp.sum(prod.reshape(ny // 8, 8, nx), axis=0)
        prod = sum(prod[:, n : n + LANES] for n in range(0, nx, LANES))
        return jnp.sum(prod, axis=0, keepdims=True)

    w0 = widened(0)
    w1 = operate(w0)
    w2 = operate(w1)
    w3 = operate(w2)
    v1r[...] = w1[:ny, :nx]
    v2r[...] = w2[:ny, :nx]
    pairs = ((w0, w0), (w0, w1), (w1, w1), (w1, w2), (w2, w2), (w2, w3))
    mom[...] = jnp.concatenate([moment(a, b) for a, b in pairs] + [jnp.zeros((2, LANES), f32)], axis=0)

    for dy, dx in others:
        send(mom, gath.at[me], gsend, grecv, neighbour(dy, dx))
    gath[me] = mom[...]
    tracer_pass(SPLIT, nlev)
    for copy in edge + rim_fixed + rim_force:
        copy.wait_send()
    for copy in outs:
        copy.wait()
    every = gath.at[pl.ds(0, total - 1)]
    pltpu.make_async_copy(every, every, grecv).wait()
    whole = jnp.sum(jnp.sum(gath[...], axis=0), axis=1, keepdims=True)
    moments = [jnp.broadcast_to(whole[n : n + 1], (8, LANES)) for n in range(6)]
    weights = [jnp.concatenate([x] * (nx // LANES), axis=1) for x in iterate_weights(moments)]
    for r in range(0, ny, 8):
        rows = slice(r, r + 8)
        surf[rows, :] = weights[0] * fld[0, rows, :] + weights[1] * v1r[rows, :] + weights[2] * v2r[rows, :]
    pltpu.make_async_copy(every, every, gsend).wait()


def on_device(nby, nbx, t1, t2, u, v, lev, side, vert, thick, cd, dg):
    nlev, ny, nx = t1.shape
    anywhere = pl.BlockSpec(memory_space=pl.ANY)
    vmem = pltpu.VMEM
    dma = pltpu.SemaphoreType.DMA
    cells = nlev * ny * nx
    made = pl.pallas_call(
        functools.partial(kernel, nby, nbx, nlev),
        out_shape=(
            jax.ShapeDtypeStruct(t1.shape, f32),
            jax.ShapeDtypeStruct(t1.shape, f32),
            jax.ShapeDtypeStruct((ny, nx), f32),
        ),
        in_specs=[anywhere] * 10,
        out_specs=(anywhere, anywhere, pl.BlockSpec(memory_space=vmem)),
        scratch_shapes=[pltpu.SMEM((nlev,), f32)] * 3
        + [
            vmem((2, nlev, ny, nx), f32),
            vmem((nlev, ny, nx), u.dtype),
            vmem((nlev, ny, nx), v.dtype),
            vmem((ny, nx), jnp.int32),
            vmem((2, nlev, ny, nx), f32),
            vmem((80, nx), f32),
            vmem((80, nx), f32),
            vmem((80, nx), f32),
            vmem((80, nx), f32),
            vmem((ny, LANES), f32),
            vmem((ny, LANES), f32),
            vmem((ny, LANES), f32),
            vmem((ny, LANES), f32),
            vmem((3, ny, nx), f32),
            vmem((3, ny, nx), f32),
            vmem((2, ny, nx), f32),
            vmem((2, 24, nx), f32),
            vmem((2, 24, nx), f32),
            vmem((2, ny, LANES), f32),
            vmem((3, ny, nx), f32),
            vmem((3, 8, nx), f32),
            vmem((3, 8, nx), f32),
            vmem((3, ny, LANES), f32),
            vmem((3, ny, LANES), f32),
            vmem((4, 3, 8, LANES), f32),
            vmem((ny, nx), f32),
            vmem((ny, nx), f32),
            vmem((8, LANES), f32),
            vmem((nby * nbx, 8, LANES), f32),
            dma((14,)),
            dma((4,)),
            dma((4,)),
            dma((4,)),
            dma((8,)),
            dma((8,)),
            dma((8,)),
            dma((8,)),
            dma,
            dma,
        ],
        compiler_params=pltpu.CompilerParams(
            collective_id=0, has_side_effects=True, vmem_limit_bytes=VMEM_MIB * 2**20
        ),
        cost_estimate=pl.CostEstimate(flops=60 * cells, bytes_accessed=20 * cells, transcendentals=0),
    )(side, vert, thick, t1, t2, u, v, lev, cd, dg)

    return pl.pallas_call(
        hand_on,
        out_shape=tuple(jax.ShapeDtypeStruct(x.shape, x.dtype) for x in made),
        in_specs=[anywhere] * 3,
        out_specs=(anywhere,) * 3,
        scratch_shapes=[vmem((2, nlev, ny, nx), f32), vmem((ny, nx), f32), dma((2, 2 * PARTS + 1))],
        compiler_params=pltpu.CompilerParams(vmem_limit_bytes=VMEM_MIB * 2**20),
        cost_estimate=pl.CostEstimate(flops=0, bytes_accessed=16 * cells, transcendentals=0),
    )(*made)


def hand_on(a, b, c, a_out, b_out, c_out, stage, plane, sems):
    step = a.shape[0] // PARTS
    moves = [(c, plane, c_out)]
    for n in range(PARTS):
        span = pl.ds(n * step, step)
        moves.append((a.at[span], stage.at[0, span], a_out.at[span]))
        moves.append((b.at[span], stage.at[1, span], b_out.at[span]))
    ins = [pltpu.make_async_copy(src, via, sems.at[0, n]) for n, (src, via, _) in enumerate(moves)]
    outs = [pltpu.make_async_copy(via, dst, sems.at[1, n]) for n, (_, via, dst) in enumerate(moves)]
    for copy in ins:
        copy.start()
    for come, go in zip(ins, outs):
        come.wait()
        go.start()
    for copy in outs:
        copy.wait()


def solution(mesh):
    def body(t1, t2, u, v, lev, side, vert, thick, cd, dg):
        return on_device(mesh.shape["by"], mesh.shape["bx"], t1, t2, u, v, lev, side, vert, thick, cd, dg)

    block, plane = P(None, "by", "bx"), P("by", "bx")
    return jax.shard_map(
        body,
        mesh=mesh,
        in_specs=(block, block, block, block, plane, P(), P(), P(), plane, plane),
        out_specs=(block, block, plane),
        check_vma=False,
    )
```

```python
import functools

import jax
import jax.numpy as jnp
from jax import lax
from jax.experimental import pallas as pl
from jax.experimental.pallas import tpu as pltpu
from jax.sharding import PartitionSpec as P

ITERS = 3
SHIFT = 3.0
CHUNK = 16
WIDE = 16
PARTS = 3
EARLY = 6
SPLIT = 8
VMEM_MIB = 62
LANES = 128
MESH = pl.DeviceIdType.MESH
f32 = jnp.float32
SIDES = ((1, 0), (-1, 0), (0, 1), (0, -1), (1, 1), (1, -1), (-1, 1), (-1, -1))


def iterate_weights(moments):
    def add(a, b, scale):
        longer = max(len(a), len(b))
        out = []
        for n in range(longer):
            if n >= len(a):
                out.append(scale * b[n])
            elif n >= len(b):
                out.append(a[n])
            else:
                out.append(a[n] + scale * b[n])
        return out

    def operate(a):
        shifted = [SHIFT * x for x in a] + [None]
        for n, x in enumerate(a):
            shifted[n + 1] = x if shifted[n + 1] is None else shifted[n + 1] + x
        return shifted

    def dot(a, b):
        total = None
        for i, x in enumerate(a):
            for j, y in enumerate(b):
                term = x * y * moments[i + j]
                total = term if total is None else total + term
        return total

    residual = [jnp.ones_like(moments[0])]
    image = operate(residual)
    now = dot(residual, residual)
    alpha = now / dot(residual, image)
    direction, along = residual, image
    surface = [jnp.zeros_like(moments[0])]
    for step in range(ITERS):
        surface = add(surface, direction, alpha)
        if step + 1 < ITERS:
            residual = add(residual, along, -alpha)
            image = operate(residual)
            new = dot(residual, residual)
            product = dot(residual, image)
            ratio = new / now
            alpha = new / (product - ratio * new / alpha)
            direction = add(residual, direction, ratio)
            along = add(image, along, ratio)
            now = new
    return surface


def kernel(
    nby, nbx, nlev,
    sideh, verth, thickh, t1h, t2h, uh, vh, levh, cdh, dgh,
    o1h, o2h, surf,
    side, vert, thick, t, u, v, levi, o, row_up, row_dn, got_dn, got_up, col_rt, col_lf, got_lf, got_rt,
    lv, sums, fall_in, flx, rows_up, cols, fld, h_up, h_dn, h_rt, h_lf, narrow, h_cn, v1r, v2r, mom, gath,
    load_sem, out_sem, send_a, recv_a, send_b, recv_b, send_c, recv_c, gsend, grecv,
):
    by, bx = lax.axis_index("by"), lax.axis_index("bx")
    total = nby * nbx
    me = by * nbx + bx
    ny, nx = fld.shape[1], fld.shape[2]

    def neighbour(dy, dx):
        y, x = by + dy % nby, bx + dx % nbx
        return (jnp.where(y >= nby, y - nby, y), jnp.where(x >= nbx, x - nbx, x))

    others = [(dy, dx) for dy in range(nby) for dx in range(nbx)][1:]
    barrier = pltpu.get_barrier_semaphore()
    for dy, dx in others:
        pl.semaphore_signal(barrier, inc=1, device_id=neighbour(dy, dx), device_id_type=MESH)

    loads = [
        pltpu.make_async_copy(sideh, side, load_sem.at[8]),
        pltpu.make_async_copy(verth, vert, load_sem.at[9]),
        pltpu.make_async_copy(thickh, thick, load_sem.at[10]),
        pltpu.make_async_copy(levh, levi, load_sem.at[11]),
    ]
    groups = ((0, EARLY), (EARLY, nlev))
    bulk = []
    for g, (first, end) in enumerate(groups):
        span = pl.ds(first, end - first)
        bulk.append([
            pltpu.make_async_copy(t1h.at[span], t.at[0, span], load_sem.at[4 * g]),
            pltpu.make_async_copy(t2h.at[span], t.at[1, span], load_sem.at[4 * g + 1]),
            pltpu.make_async_copy(uh.at[span], u.at[span], load_sem.at[4 * g + 2]),
            pltpu.make_async_copy(vh.at[span], v.at[span], load_sem.at[4 * g + 3]),
        ])
    planes = [
        pltpu.make_async_copy(cdh, fld.at[1], load_sem.at[12]),
        pltpu.make_async_copy(dgh, fld.at[2], load_sem.at[13]),
    ]
    for copy in loads + bulk[0] + bulk[1] + planes:
        copy.start()

    up_ok = jnp.where(by < nby - 1, 1.0, 0.0).astype(f32)
    dn_ok = jnp.where(by > 0, 1.0, 0.0).astype(f32)

    for copy in loads:
        copy.wait()
    levels = levi[...]
    levf = levels.astype(f32)

    sub_c = lax.broadcasted_iota(jnp.int32, (CHUNK, nx), 0)
    lane_c = lax.broadcasted_iota(jnp.int32, (CHUNK, nx), 1)
    for r in range(0, ny, CHUNK):
        rows = slice(r, r + CHUNK)
        lev = levf[rows]
        lev_rt = jnp.where(lane_c == nx - 1, 0.0, pltpu.roll(lev, nx - 1, 1))
        above = levf[r + CHUNK : r + CHUNK + 1] if r + CHUNK < ny else 0.0
        lev_up = jnp.where(sub_c == CHUNK - 1, above, pltpu.roll(lev, CHUNK - 1, 0))
        lv[0, rows, :] = lev
        lv[1, rows, :] = jnp.minimum(lev, lev_rt)
        lv[2, rows, :] = jnp.minimum(lev, lev_up)
    def force_pass(g):
        start, end = groups[g]

        def rows_of(n, _):
            r = pl.multiple_of(n * CHUNK, CHUNK)
            rows = pl.ds(r, CHUNK)
            above = jnp.minimum(r + CHUNK, ny - 1)
            lev, lev_e, lev_n = lv[0, rows, :], lv[1, rows, :], lv[2, rows, :]
            before = None
            if start:
                before = t[0, start - 1, rows, :] - 0.5 * t[1, start - 1, rows, :]
                acc = [sums[m, rows, :] for m in range(3)]
            else:
                acc = [jnp.zeros((CHUNK, nx), f32)] * 3
            for k in range(start, end):
                g_here = t[0, k, rows, :] - 0.5 * t[1, k, rows, :]
                top = t[0, k, pl.ds(above, 1), :] - 0.5 * t[1, k, pl.ds(above, 1), :]
                g_up = jnp.where(sub_c == CHUNK - 1, top, pltpu.roll(g_here, CHUNK - 1, 0))
                g_rt = pltpu.roll(g_here, nx - 1, 1)
                twice = 2.0 * side[k]
                east = u[k, rows, :].astype(f32) * (g_here + g_rt) - twice * (g_rt - g_here)
                north = v[k, rows, :].astype(f32) * (g_here + g_up) - twice * (g_up - g_here)
                inside = thick[k] * g_here
                if k:
                    inside = inside + (vert[k - 1] * (thick[k - 1] - thick[k])) * (g_here - before)
                half = 0.5 * thick[k]
                acc[0] = acc[0] + jnp.where(lev > k, inside, 0.0)
                acc[1] = acc[1] + half * jnp.where(lev_e > k, east, 0.0)
                acc[2] = acc[2] + half * jnp.where(lev_n > k, north, 0.0)
                before = g_here
            for m in range(3):
                sums[m, rows, :] = acc[m]
            return 0

        lax.fori_loop(0, ny // CHUNK, rows_of, 0)

    for copy in bulk[0]:
        copy.wait()
    force_pass(0)
    for copy in bulk[1]:
        copy.wait()

    lane = lax.broadcasted_iota(jnp.int32, (ny, LANES), 1)
    row_up[pl.ds(48, 8), :] = jnp.broadcast_to(levf[ny - 1 : ny], (8, nx))
    row_dn[pl.ds(48, 8), :] = jnp.broadcast_to(levf[0:1], (8, nx))
    right = jnp.where(lane == 96, pltpu.roll(levf[:, nx - LANES :], 97, 1), 0.0)
    left = jnp.where(lane == 96, pltpu.roll(levf[:, :LANES], 96, 1), 0.0)
    for c in range(2):
        for k in range(nlev):
            place = 32 * c + k
            right = jnp.where(lane == place, pltpu.roll(t[c, k, :, nx - LANES :], place + 1, 1), right)
            tile = t[c, k, :, :LANES]
            left = jnp.where(lane == place, pltpu.roll(tile, place, 1) if place else tile, left)
    for k in range(nlev):
        right = jnp.where(lane == 64 + k, pltpu.roll(u[k, :, nx - LANES :].astype(f32), 65 + k, 1), right)
    for c in range(2):
        upper = [t[c, k, ny - 1 : ny, :] for k in range(nlev)]
        lower = [t[c, k, 0:1, :] for k in range(nlev)]
        for k in range(nlev):
            row_up[24 * c + k : 24 * c + k + 1, :] = upper[k]
            row_dn[24 * c + k : 24 * c + k + 1, :] = lower[k]
    upper = [v[k, ny - 16 :, :].astype(f32)[15:16] for k in range(nlev)]
    for k in range(nlev):
        row_up[56 + k : 57 + k, :] = upper[k]
    col_rt[...] = right
    col_lf[...] = left

    pl.semaphore_wait(barrier, total - 1)

    def send(src, dst, ssem, rsem, to):
        copy = pltpu.make_async_remote_copy(
            src_ref=src, dst_ref=dst, send_sem=ssem, recv_sem=rsem, device_id=to, device_id_type=MESH
        )
        copy.start()
        return copy

    edge = [
        send(row_up, got_dn, send_a.at[0], recv_a.at[0], neighbour(1, 0)),
        send(row_dn, got_up, send_a.at[1], recv_a.at[1], neighbour(-1, 0)),
        send(col_rt, got_lf, send_a.at[2], recv_a.at[2], neighbour(0, 1)),
        send(col_lf, got_rt, send_a.at[3], recv_a.at[3], neighbour(0, -1)),
    ]

    lane_8 = lane[:8]

    def fold(n):
        right = left = jnp.zeros((8, LANES), f32)
        for g in range(ny // 8):
            rows = slice(8 * g, 8 * g + 8)
            mine = (lane_8 >= WIDE * g) & (lane_8 < WIDE * g + WIDE)
            right = jnp.where(mine, pltpu.roll(fld[n, rows, nx - LANES :], (WIDE * g + WIDE) % LANES, 1), right)
            tile = fld[n, rows, :LANES]
            left = jnp.where(mine, pltpu.roll(tile, WIDE * g, 1) if g else tile, left)
        narrow[0, n] = right
        narrow[1, n] = left

    def rim(which, ssem, rsem):
        copies = []
        for n, (dy, dx) in enumerate(SIDES):
            rows = pl.ds(ny - 8, 8) if dy > 0 else pl.ds(0, 8)
            cols = pl.ds(0, nx) if dx == 0 else (pl.ds(nx - LANES, LANES) if dx > 0 else pl.ds(0, LANES))
            place = {0: h_dn, 1: h_up, 2: h_lf, 3: h_rt}.get(n)
            dst = h_cn.at[n - 4, which] if place is None else place.at[which]
            src = fld.at[which, rows, cols] if dy else narrow.at[n - 2, which]
            copies.append(send(src, dst, ssem.at[n], rsem.at[n], neighbour(dy, dx)))
        return copies

    for copy in planes:
        copy.wait()
    fld[1] = fld[1] * jnp.where(levels > 0, 0.5, 0.0).astype(f32)
    fld[2] = fld[2] - SHIFT
    fold(1)
    fold(2)
    rim_fixed = rim(pl.ds(1, 2), send_b, recv_b)

    force_pass(1)
    force = sums[0] + (pltpu.roll(sums[1], 1, 1) - sums[1]) + (pltpu.roll(sums[2], 1, 0) - sums[2])
    fld[0] = force

    k_sub = lax.broadcasted_iota(jnp.int32, (24, nx), 0)
    k_lane = lax.rem(lane, 32)
    side_sub = jnp.zeros((24, nx), f32)
    thick_sub = jnp.zeros((24, nx), f32)
    side_lane = jnp.zeros((8, LANES), f32)
    thick_lane = jnp.zeros((8, LANES), f32)
    for k in range(nlev):
        side_sub = jnp.where(k_sub == k, side[k], side_sub)
        thick_sub = jnp.where(k_sub == k, thick[k], thick_sub)
        side_lane = jnp.where(k_lane[:8] == k, side[k], side_lane)
        thick_lane = jnp.where(lane[:8] == k, thick[k], thick_lane)
        thick_lane = jnp.where(lane[:8] == 32 + k, -0.5 * thick[k], thick_lane)
    side_lane, thick_lane = (jnp.concatenate([x] * (ny // 8), axis=0) for x in (side_lane, thick_lane))

    for copy in edge:
        copy.wait_recv()

    def row_flux(lower, upper, ok):
        lowest = jnp.minimum(lower[48:49, :], upper[48:49, :]) * ok
        is_open = k_sub.astype(f32) < lowest
        half = 0.5 * lower[56:80, :]
        p, q = jnp.where(is_open, half + side_sub, 0.0), jnp.where(is_open, half - side_sub, 0.0)
        out = []
        for c in range(2):
            flux = p * lower[24 * c : 24 * c + 24, :] + q * upper[24 * c : 24 * c + 24, :]
            out.append(jnp.where(is_open, flux, 0.0))
        return out

    def col_flux(came, beyond):
        half = 0.5 * jnp.where(lane < 32, pltpu.roll(came, 64, 1), pltpu.roll(came, 96, 1))
        lowest = jnp.minimum(came[:, 96:97], beyond[:, 96:97])
        flux = (half + side_lane) * came + (half - side_lane) * beyond
        return jnp.where(k_lane.astype(f32) < lowest, flux, 0.0)

    flux_dn = row_flux(got_dn, row_dn, dn_ok)
    flux_up = row_flux(row_up, got_up, up_ok)
    flux_lf = col_flux(got_lf[...], col_lf[...])
    flux_rt = col_flux(col_rt[...], got_rt[...])

    def weighed(flux):
        return jnp.sum(thick_sub * (flux[0] - 0.5 * flux[1]), axis=0, keepdims=True)

    fld[0, 0:1, :] += weighed(flux_dn)
    fld[0, ny - 1 : ny, :] -= weighed(flux_up)
    fld[0, :, :LANES] += jnp.where(lane == 0, jnp.sum(thick_lane * flux_lf, axis=1, keepdims=True), 0.0)
    fld[0, :, nx - LANES :] -= jnp.where(lane == LANES - 1, jnp.sum(thick_lane * flux_rt, axis=1, keepdims=True), 0.0)
    fold(0)
    rim_force = rim(0, send_c, recv_c)

    outs = []
    for c in range(2):
        flx[c] = flux_dn[c]
        rows_up[c] = flux_up[c]
    cols[0] = flux_lf
    cols[1] = flux_rt
    fall_in[...] = jnp.zeros_like(fall_in)
    lane_t = lane[:CHUNK]

    def tracer_pass(first, end):
        def rows_of(n, _):
            r = pl.multiple_of(n * CHUNK, CHUNK)
            rows = pl.ds(r, CHUNK)
            above = jnp.minimum(r + CHUNK, ny - 1)
            lev, lev_e, lev_n = lv[0, rows, :], lv[1, rows, :], lv[2, rows, :]
            from_lf, from_rt = cols[0, rows, :], cols[1, rows, :]
            falls = [fall_in[c, rows, :] for c in range(2)]
            pending = []
            for k in range(first, end):
                here = [t[c, k, rows, :] for c in range(2)]
                top = [t[c, k, pl.ds(above, 1), :] for c in range(2)]
                under = [flx[c, k : k + 1, :] for c in range(2)]
                below = [t[c, k + 1, rows, :] for c in range(2)] if k + 1 < nlev else None
                hu = 0.5 * u[k, rows, :].astype(f32)
                hv = 0.5 * v[k, rows, :].astype(f32)
                for ref, where, value in pending:
                    ref[where] = value
                pending = []
                s = side[k]
                in_e, in_n = lev_e > k, lev_n > k
                pe, qe = jnp.where(in_e, hu + s, 0.0), jnp.where(in_e, hu - s, 0.0)
                pn, qn = jnp.where(in_n, hv + s, 0.0), jnp.where(in_n, hv - s, 0.0)
                wet = lev > k
                if k + 1 < nlev:
                    fall_w = jnp.where(lev > k + 1, vert[k], 0.0)
                for c in range(2):
                    x = here[c]
                    up = jnp.where(sub_c == CHUNK - 1, top[c], pltpu.roll(x, CHUNK - 1, 0))
                    east = pe * x + qe * pltpu.roll(x, nx - 1, 1)
                    north = pn * x + qn * up
                    south = jnp.where(sub_c == 0, under[c], pltpu.roll(north, 1, 0))
                    place = 32 * c + k
                    lf = pltpu.roll(from_lf, LANES - place, 1) if place else from_lf
                    rt = pltpu.roll(from_rt, LANES - 1 - place, 1)
                    shared = jnp.concatenate(
                        [jnp.where(lane_t == 0, lf, 0.0)]
                        + [jnp.zeros((CHUNK, LANES), f32)] * (nx // LANES - 2)
                        + [jnp.where(lane_t == LANES - 1, -rt, 0.0)],
                        axis=1,
                    )
                    new = x + (pltpu.roll(east, 1, 1) - east + shared) + (south - north) - falls[c]
                    if k + 1 < nlev:
                        falls[c] = fall_w * (below[c] - x)
                        new = new + falls[c]
                    pending.append((o, (c, k, rows), jnp.where(wet, new, 0.0)))
                    pending.append((flx, (c, slice(k, k + 1)), north[CHUNK - 1 :]))
            for ref, where, value in pending:
                ref[where] = value
            for c in range(2):
                fall_in[c, rows, :] = falls[c]
            return 0

        lax.fori_loop(0, ny // CHUNK, rows_of, 0)
        span = pl.ds(first, end - first)
        for c, dst in enumerate((o1h, o2h)):
            ends = [o[c, k, ny - 1 : ny, :] - rows_up[c, k : k + 1, :] for k in range(first, end)]
            for k in range(first, end):
                o[c, k, ny - 1 : ny, :] = ends[k - first]
            copy = pltpu.make_async_copy(o.at[c, span], dst.at[span], out_sem.at[len(outs)])
            copy.start()
            outs.append(copy)

    tracer_pass(0, SPLIT)

    sub8 = lax.broadcasted_iota(jnp.int32, (8, nx), 0) < 4
    sub8c = sub8[:, :LANES]
    lane8 = lax.broadcasted_iota(jnp.int32, (8, LANES), 1) < 64
    row = lax.broadcasted_iota(jnp.int32, (ny + 8, nx + LANES), 0)
    mask = jnp.where(row < ny, 1.0, jnp.where(row < ny + 4, up_ok, dn_ok)).astype(f32)

    def widened(n):
        pieces = []
        for g in range(ny // 8):
            right = pltpu.roll(h_rt[n], LANES - WIDE * g, 1) if g else h_rt[n]
            shift = (LANES - WIDE - WIDE * g) % LANES
            left = pltpu.roll(h_lf[n], shift, 1) if shift else h_lf[n]
            pieces.append(jnp.where(lane8, right, left))
        beside = jnp.concatenate(pieces, axis=0)
        ends = jnp.where(sub8, h_up[n], h_dn[n])
        corner = jnp.where(
            sub8c, jnp.where(lane8, h_cn[3, n], h_cn[2, n]), jnp.where(lane8, h_cn[1, n], h_cn[0, n])
        )
        top = jnp.concatenate([fld[n], beside], axis=1)
        bottom = jnp.concatenate([ends, corner], axis=1)
        return jnp.concatenate([top, bottom], axis=0) * mask

    for copy in rim_fixed:
        copy.wait_recv()
    depth, diag = widened(1), widened(2)
    for copy in rim_force:
        copy.wait_recv()
    tall, wide = ny + 8, nx + LANES

    def operate(a):
        b = pltpu.roll(a, wide - 1, 1)
        cc = pltpu.roll(a, tall - 1, 0)
        d = pltpu.roll(b, tall - 1, 0)
        p = depth * (d - a)
        q = depth * (b - cc)
        return (diag * a - p + pltpu.roll(q, 1, 1) + pltpu.roll(pltpu.roll(p, 1, 1) - q, 1, 0)) * mask

    def moment(a, b):
        prod = a[:ny, :nx] * b[:ny, :nx]
        prod = jnp.sum(prod.reshape(ny // 8, 8, nx), axis=0)
        prod = sum(prod[:, n : n + LANES] for n in range(0, nx, LANES))
        return jnp.sum(prod, axis=0, keepdims=True)

    w0 = widened(0)
    w1 = operate(w0)
    w2 = operate(w1)
    w3 = operate(w2)
    v1r[...] = w1[:ny, :nx]
    v2r[...] = w2[:ny, :nx]
    pairs = ((w0, w0), (w0, w1), (w1, w1), (w1, w2), (w2, w2), (w2, w3))
    mom[...] = jnp.concatenate([moment(a, b) for a, b in pairs] + [jnp.zeros((2, LANES), f32)], axis=0)

    for dy, dx in others:
        send(mom, gath.at[me], gsend, grecv, neighbour(dy, dx))
    gath[me] = mom[...]
    tracer_pass(SPLIT, nlev)
    for copy in edge + rim_fixed + rim_force:
        copy.wait_send()
    for copy in outs:
        copy.wait()
    every = gath.at[pl.ds(0, total - 1)]
    pltpu.make_async_copy(every, every, grecv).wait()
    whole = jnp.sum(jnp.sum(gath[...], axis=0), axis=1, keepdims=True)
    moments = [jnp.broadcast_to(whole[n : n + 1], (8, LANES)) for n in range(6)]
    weights = [jnp.concatenate([x] * (nx // LANES), axis=1) for x in iterate_weights(moments)]
    for r in range(0, ny, 8):
        rows = slice(r, r + 8)
        surf[rows, :] = weights[0] * fld[0, rows, :] + weights[1] * v1r[rows, :] + weights[2] * v2r[rows, :]
    pltpu.make_async_copy(every, every, gsend).wait()


def on_device(nby, nbx, t1, t2, u, v, lev, side, vert, thick, cd, dg):
    nlev, ny, nx = t1.shape
    anywhere = pl.BlockSpec(memory_space=pl.ANY)
    vmem = pltpu.VMEM
    dma = pltpu.SemaphoreType.DMA
    cells = nlev * ny * nx
    made = pl.pallas_call(
        functools.partial(kernel, nby, nbx, nlev),
        out_shape=(
            jax.ShapeDtypeStruct(t1.shape, f32),
            jax.ShapeDtypeStruct(t1.shape, f32),
            jax.ShapeDtypeStruct((ny, nx), f32),
        ),
        in_specs=[anywhere] * 10,
        out_specs=(anywhere, anywhere, pl.BlockSpec(memory_space=vmem)),
        scratch_shapes=[pltpu.SMEM((nlev,), f32)] * 3
        + [
            vmem((2, nlev, ny, nx), f32),
            vmem((nlev, ny, nx), u.dtype),
            vmem((nlev, ny, nx), v.dtype),
            vmem((ny, nx), jnp.int32),
            vmem((2, nlev, ny, nx), f32),
            vmem((80, nx), f32),
            vmem((56, nx), f32),
            vmem((80, nx), f32),
            vmem((56, nx), f32),
            vmem((ny, LANES), f32),
            vmem((ny, LANES), f32),
            vmem((ny, LANES), f32),
            vmem((ny, LANES), f32),
            vmem((3, ny, nx), f32),
            vmem((3, ny, nx), f32),
            vmem((2, ny, nx), f32),
            vmem((2, 24, nx), f32),
            vmem((2, 24, nx), f32),
            vmem((2, ny, LANES), f32),
            vmem((3, ny, nx), f32),
            vmem((3, 8, nx), f32),
            vmem((3, 8, nx), f32),
            vmem((3, 8, LANES), f32),
            vmem((3, 8, LANES), f32),
            vmem((2, 3, 8, LANES), f32),
            vmem((4, 3, 8, LANES), f32),
            vmem((ny, nx), f32),
            vmem((ny, nx), f32),
            vmem((8, LANES), f32),
            vmem((nby * nbx, 8, LANES), f32),
            dma((14,)),
            dma((4,)),
            dma((4,)),
            dma((4,)),
            dma((8,)),
            dma((8,)),
            dma((8,)),
            dma((8,)),
            dma,
            dma,
        ],
        compiler_params=pltpu.CompilerParams(
            collective_id=0, has_side_effects=True, vmem_limit_bytes=VMEM_MIB * 2**20
        ),
        cost_estimate=pl.CostEstimate(flops=60 * cells, bytes_accessed=20 * cells, transcendentals=0),
    )(side, vert, thick, t1, t2, u, v, lev, cd, dg)

    return pl.pallas_call(
        hand_on,
        out_shape=tuple(jax.ShapeDtypeStruct(x.shape, x.dtype) for x in made),
        in_specs=[anywhere] * 3,
        out_specs=(anywhere,) * 3,
        scratch_shapes=[vmem((2, nlev, ny, nx), f32), vmem((ny, nx), f32), dma((2, 2 * PARTS + 1))],
        compiler_params=pltpu.CompilerParams(vmem_limit_bytes=VMEM_MIB * 2**20),
        cost_estimate=pl.CostEstimate(flops=0, bytes_accessed=16 * cells, transcendentals=0),
    )(*made)


def hand_on(a, b, c, a_out, b_out, c_out, stage, plane, sems):
    step = a.shape[0] // PARTS
    moves = [(c, plane, c_out)]
    for n in range(PARTS):
        span = pl.ds(n * step, step)
        moves.append((a.at[span], stage.at[0, span], a_out.at[span]))
        moves.append((b.at[span], stage.at[1, span], b_out.at[span]))
    ins = [pltpu.make_async_copy(src, via, sems.at[0, n]) for n, (src, via, _) in enumerate(moves)]
    outs = [pltpu.make_async_copy(via, dst, sems.at[1, n]) for n, (_, via, dst) in enumerate(moves)]
    for copy in ins:
        copy.start()
    for come, go in zip(ins, outs):
        come.wait()
        go.start()
    for copy in outs:
        copy.wait()


def solution(mesh):
    def body(t1, t2, u, v, lev, side, vert, thick, cd, dg):
        return on_device(mesh.shape["by"], mesh.shape["bx"], t1, t2, u, v, lev, side, vert, thick, cd, dg)

    block, plane = P(None, "by", "bx"), P("by", "bx")
    return jax.shard_map(
        body,
        mesh=mesh,
        in_specs=(block, block, block, block, plane, P(), P(), P(), plane, plane),
        out_specs=(block, block, plane),
        check_vma=False,
    )
```

```python
import functools

import jax
import jax.numpy as jnp
from jax import lax
from jax.experimental import pallas as pl
from jax.experimental.pallas import tpu as pltpu
from jax.sharding import PartitionSpec as P

ITERS = 3
SHIFT = 3.0
CHUNK = 16
WIDE = 16
PARTS = 6
EARLY = 6
SPLIT = 8
SECOND = 11
VMEM_MIB = 62
LANES = 128
MESH = pl.DeviceIdType.MESH
f32 = jnp.float32
SIDES = ((1, 0), (-1, 0), (0, 1), (0, -1), (1, 1), (1, -1), (-1, 1), (-1, -1))


def iterate_weights(moments):
    def add(a, b, scale):
        longer = max(len(a), len(b))
        out = []
        for n in range(longer):
            if n >= len(a):
                out.append(scale * b[n])
            elif n >= len(b):
                out.append(a[n])
            else:
                out.append(a[n] + scale * b[n])
        return out

    def operate(a):
        shifted = [SHIFT * x for x in a] + [None]
        for n, x in enumerate(a):
            shifted[n + 1] = x if shifted[n + 1] is None else shifted[n + 1] + x
        return shifted

    def dot(a, b):
        total = None
        for i, x in enumerate(a):
            for j, y in enumerate(b):
                term = x * y * moments[i + j]
                total = term if total is None else total + term
        return total

    residual = [jnp.ones_like(moments[0])]
    image = operate(residual)
    now = dot(residual, residual)
    alpha = now / dot(residual, image)
    direction, along = residual, image
    surface = [jnp.zeros_like(moments[0])]
    for step in range(ITERS):
        surface = add(surface, direction, alpha)
        if step + 1 < ITERS:
            residual = add(residual, along, -alpha)
            image = operate(residual)
            new = dot(residual, residual)
            product = dot(residual, image)
            ratio = new / now
            alpha = new / (product - ratio * new / alpha)
            direction = add(residual, direction, ratio)
            along = add(image, along, ratio)
            now = new
    return surface


def kernel(
    nby, nbx, nlev,
    sideh, verth, thickh, t1h, t2h, uh, vh, levh, cdh, dgh,
    o1h, o2h, surf,
    side, vert, thick, t, u, v, levi, o, row_up, row_dn, got_dn, got_up, col_rt, col_lf, got_lf, got_rt,
    lv, sums, fall_in, flx, rows_up, cols, fld, h_up, h_dn, h_rt, h_lf, narrow, h_cn, v1r, v2r, mom, part, gath_by, gath,
    load_sem, out_sem, send_a, recv_a, send_b, recv_b, send_c, recv_c, gsend, grecv,
):
    by, bx = lax.axis_index("by"), lax.axis_index("bx")
    ny, nx = fld.shape[1], fld.shape[2]

    def neighbour(dy, dx):
        y, x = by + dy % nby, bx + dx % nbx
        return (jnp.where(y >= nby, y - nby, y), jnp.where(x >= nbx, x - nbx, x))

    column = [(dy, 0) for dy in range(1, nby)]
    line = [(0, dx) for dx in range(1, nbx)]
    partners = column + line + [(dy, dx) for dy, dx in SIDES if dy and dx]
    barrier = pltpu.get_barrier_semaphore()
    for dy, dx in partners:
        pl.semaphore_signal(barrier, inc=1, device_id=neighbour(dy, dx), device_id_type=MESH)

    loads = [
        pltpu.make_async_copy(sideh, side, load_sem.at[8]),
        pltpu.make_async_copy(verth, vert, load_sem.at[9]),
        pltpu.make_async_copy(thickh, thick, load_sem.at[10]),
        pltpu.make_async_copy(levh, levi, load_sem.at[11]),
    ]
    groups = ((0, EARLY), (EARLY, nlev))
    bulk = []
    for g, (first, end) in enumerate(groups):
        span = pl.ds(first, end - first)
        bulk.append([
            pltpu.make_async_copy(t1h.at[span], t.at[0, span], load_sem.at[4 * g]),
            pltpu.make_async_copy(t2h.at[span], t.at[1, span], load_sem.at[4 * g + 1]),
            pltpu.make_async_copy(uh.at[span], u.at[span], load_sem.at[4 * g + 2]),
            pltpu.make_async_copy(vh.at[span], v.at[span], load_sem.at[4 * g + 3]),
        ])
    planes = [
        pltpu.make_async_copy(cdh, fld.at[1], load_sem.at[12]),
        pltpu.make_async_copy(dgh, fld.at[2], load_sem.at[13]),
    ]
    for copy in loads + bulk[0] + bulk[1] + planes:
        copy.start()

    up_ok = jnp.where(by < nby - 1, 1.0, 0.0).astype(f32)
    dn_ok = jnp.where(by > 0, 1.0, 0.0).astype(f32)

    for copy in loads:
        copy.wait()
    levels = levi[...]
    levf = levels.astype(f32)

    sub_c = lax.broadcasted_iota(jnp.int32, (CHUNK, nx), 0)
    lane_c = lax.broadcasted_iota(jnp.int32, (CHUNK, nx), 1)
    for r in range(0, ny, CHUNK):
        rows = slice(r, r + CHUNK)
        lev = levf[rows]
        lev_rt = jnp.where(lane_c == nx - 1, 0.0, pltpu.roll(lev, nx - 1, 1))
        above = levf[r + CHUNK : r + CHUNK + 1] if r + CHUNK < ny else 0.0
        lev_up = jnp.where(sub_c == CHUNK - 1, above, pltpu.roll(lev, CHUNK - 1, 0))
        lv[0, rows, :] = lev
        lv[1, rows, :] = jnp.minimum(lev, lev_rt)
        lv[2, rows, :] = jnp.minimum(lev, lev_up)
    def force_pass(g):
        start, end = groups[g]

        def rows_of(n, _):
            r = pl.multiple_of(n * CHUNK, CHUNK)
            rows = pl.ds(r, CHUNK)
            above = jnp.minimum(r + CHUNK, ny - 1)
            lev, lev_e, lev_n = lv[0, rows, :], lv[1, rows, :], lv[2, rows, :]
            before = None
            if start:
                before = t[0, start - 1, rows, :] - 0.5 * t[1, start - 1, rows, :]
                acc = [sums[m, rows, :] for m in range(3)]
            else:
                acc = [jnp.zeros((CHUNK, nx), f32)] * 3
            for k in range(start, end):
                g_here = t[0, k, rows, :] - 0.5 * t[1, k, rows, :]
                top = t[0, k, pl.ds(above, 1), :] - 0.5 * t[1, k, pl.ds(above, 1), :]
                g_up = jnp.where(sub_c == CHUNK - 1, top, pltpu.roll(g_here, CHUNK - 1, 0))
                g_rt = pltpu.roll(g_here, nx - 1, 1)
                twice = 2.0 * side[k]
                east = u[k, rows, :].astype(f32) * (g_here + g_rt) - twice * (g_rt - g_here)
                north = v[k, rows, :].astype(f32) * (g_here + g_up) - twice * (g_up - g_here)
                inside = thick[k] * g_here
                if k:
                    inside = inside + (vert[k - 1] * (thick[k - 1] - thick[k])) * (g_here - before)
                half = 0.5 * thick[k]
                acc[0] = acc[0] + jnp.where(lev > k, inside, 0.0)
                acc[1] = acc[1] + half * jnp.where(lev_e > k, east, 0.0)
                acc[2] = acc[2] + half * jnp.where(lev_n > k, north, 0.0)
                before = g_here
            for m in range(3):
                sums[m, rows, :] = acc[m]
            return 0

        lax.fori_loop(0, ny // CHUNK, rows_of, 0)

    for copy in bulk[0] + bulk[1]:
        copy.wait()

    lane = lax.broadcasted_iota(jnp.int32, (ny, LANES), 1)
    row_up[pl.ds(48, 8), :] = jnp.broadcast_to(levf[ny - 1 : ny], (8, nx))
    row_dn[pl.ds(48, 8), :] = jnp.broadcast_to(levf[0:1], (8, nx))
    right = jnp.where(lane == 96, pltpu.roll(levf[:, nx - LANES :], 97, 1), 0.0)
    left = jnp.where(lane == 96, pltpu.roll(levf[:, :LANES], 96, 1), 0.0)
    for c in range(2):
        for k in range(nlev):
            place = 32 * c + k
            right = jnp.where(lane == place, pltpu.roll(t[c, k, :, nx - LANES :], place + 1, 1), right)
            tile = t[c, k, :, :LANES]
            left = jnp.where(lane == place, pltpu.roll(tile, place, 1) if place else tile, left)
    for k in range(nlev):
        right = jnp.where(lane == 64 + k, pltpu.roll(u[k, :, nx - LANES :].astype(f32), 65 + k, 1), right)
    for c in range(2):
        upper = [t[c, k, ny - 1 : ny, :] for k in range(nlev)]
        lower = [t[c, k, 0:1, :] for k in range(nlev)]
        for k in range(nlev):
            row_up[24 * c + k : 24 * c + k + 1, :] = upper[k]
            row_dn[24 * c + k : 24 * c + k + 1, :] = lower[k]
    upper = [v[k, ny - 16 :, :].astype(f32)[15:16] for k in range(nlev)]
    for k in range(nlev):
        row_up[56 + k : 57 + k, :] = upper[k]
    col_rt[...] = right
    col_lf[...] = left

    pl.semaphore_wait(barrier, len(partners))

    def send(src, dst, ssem, rsem, to):
        copy = pltpu.make_async_remote_copy(
            src_ref=src, dst_ref=dst, send_sem=ssem, recv_sem=rsem, device_id=to, device_id_type=MESH
        )
        copy.start()
        return copy

    edge = [
        send(row_up, got_dn, send_a.at[0], recv_a.at[0], neighbour(1, 0)),
        send(row_dn, got_up, send_a.at[1], recv_a.at[1], neighbour(-1, 0)),
        send(col_rt, got_lf, send_a.at[2], recv_a.at[2], neighbour(0, 1)),
        send(col_lf, got_rt, send_a.at[3], recv_a.at[3], neighbour(0, -1)),
    ]

    lane_8 = lane[:8]

    def fold(n):
        right = left = jnp.zeros((8, LANES), f32)
        for g in range(ny // 8):
            rows = slice(8 * g, 8 * g + 8)
            mine = (lane_8 >= WIDE * g) & (lane_8 < WIDE * g + WIDE)
            right = jnp.where(mine, pltpu.roll(fld[n, rows, nx - LANES :], (WIDE * g + WIDE) % LANES, 1), right)
            tile = fld[n, rows, :LANES]
            left = jnp.where(mine, pltpu.roll(tile, WIDE * g, 1) if g else tile, left)
        narrow[0, n] = right
        narrow[1, n] = left

    def rim(which, ssem, rsem):
        copies = []
        for n, (dy, dx) in enumerate(SIDES):
            rows = pl.ds(ny - 8, 8) if dy > 0 else pl.ds(0, 8)
            cols = pl.ds(0, nx) if dx == 0 else (pl.ds(nx - LANES, LANES) if dx > 0 else pl.ds(0, LANES))
            place = {0: h_dn, 1: h_up, 2: h_lf, 3: h_rt}.get(n)
            dst = h_cn.at[n - 4, which] if place is None else place.at[which]
            src = fld.at[which, rows, cols] if dy else narrow.at[n - 2, which]
            copies.append(send(src, dst, ssem.at[n], rsem.at[n], neighbour(dy, dx)))
        return copies

    for copy in planes:
        copy.wait()
    fld[1] = fld[1] * jnp.where(levels > 0, 0.5, 0.0).astype(f32)
    fld[2] = fld[2] - SHIFT
    fold(1)
    fold(2)
    rim_fixed = rim(pl.ds(1, 2), send_b, recv_b)

    force_pass(0)
    force_pass(1)
    force = sums[0] + (pltpu.roll(sums[1], 1, 1) - sums[1]) + (pltpu.roll(sums[2], 1, 0) - sums[2])
    fld[0] = force

    k_sub = lax.broadcasted_iota(jnp.int32, (24, nx), 0)
    k_lane = lax.rem(lane, 32)
    side_sub = jnp.zeros((24, nx), f32)
    thick_sub = jnp.zeros((24, nx), f32)
    side_lane = jnp.zeros((8, LANES), f32)
    thick_lane = jnp.zeros((8, LANES), f32)
    for k in range(nlev):
        side_sub = jnp.where(k_sub == k, side[k], side_sub)
        thick_sub = jnp.where(k_sub == k, thick[k], thick_sub)
        side_lane = jnp.where(k_lane[:8] == k, side[k], side_lane)
        thick_lane = jnp.where(lane[:8] == k, thick[k], thick_lane)
        thick_lane = jnp.where(lane[:8] == 32 + k, -0.5 * thick[k], thick_lane)
    side_lane, thick_lane = (jnp.concatenate([x] * (ny // 8), axis=0) for x in (side_lane, thick_lane))

    for copy in edge:
        copy.wait_recv()

    def row_flux(lower, upper, ok):
        lowest = jnp.minimum(lower[48:49, :], upper[48:49, :]) * ok
        is_open = k_sub.astype(f32) < lowest
        half = 0.5 * lower[56:80, :]
        p, q = jnp.where(is_open, half + side_sub, 0.0), jnp.where(is_open, half - side_sub, 0.0)
        out = []
        for c in range(2):
            flux = p * lower[24 * c : 24 * c + 24, :] + q * upper[24 * c : 24 * c + 24, :]
            out.append(jnp.where(is_open, flux, 0.0))
        return out

    def col_flux(came, beyond):
        half = 0.5 * jnp.where(lane < 32, pltpu.roll(came, 64, 1), pltpu.roll(came, 96, 1))
        lowest = jnp.minimum(came[:, 96:97], beyond[:, 96:97])
        flux = (half + side_lane) * came + (half - side_lane) * beyond
        return jnp.where(k_lane.astype(f32) < lowest, flux, 0.0)

    flux_dn = row_flux(got_dn, row_dn, dn_ok)
    flux_up = row_flux(row_up, got_up, up_ok)
    flux_lf = col_flux(got_lf[...], col_lf[...])
    flux_rt = col_flux(col_rt[...], got_rt[...])

    def weighed(flux):
        return jnp.sum(thick_sub * (flux[0] - 0.5 * flux[1]), axis=0, keepdims=True)

    fld[0, 0:1, :] += weighed(flux_dn)
    fld[0, ny - 1 : ny, :] -= weighed(flux_up)
    fld[0, :, :LANES] += jnp.where(lane == 0, jnp.sum(thick_lane * flux_lf, axis=1, keepdims=True), 0.0)
    fld[0, :, nx - LANES :] -= jnp.where(lane == LANES - 1, jnp.sum(thick_lane * flux_rt, axis=1, keepdims=True), 0.0)
    fold(0)
    rim_force = rim(0, send_c, recv_c)

    outs = []
    for c in range(2):
        flx[c] = flux_dn[c]
        rows_up[c] = flux_up[c]
    cols[0] = flux_lf
    cols[1] = flux_rt
    fall_in[...] = jnp.zeros_like(fall_in)
    lane_t = lane[:CHUNK]

    def tracer_pass(first, end):
        def rows_of(n, _):
            r = pl.multiple_of(n * CHUNK, CHUNK)
            rows = pl.ds(r, CHUNK)
            above = jnp.minimum(r + CHUNK, ny - 1)
            lev, lev_e, lev_n = lv[0, rows, :], lv[1, rows, :], lv[2, rows, :]
            from_lf, from_rt = cols[0, rows, :], cols[1, rows, :]
            falls = [fall_in[c, rows, :] for c in range(2)]
            pending = []
            for k in range(first, end):
                here = [t[c, k, rows, :] for c in range(2)]
                top = [t[c, k, pl.ds(above, 1), :] for c in range(2)]
                under = [flx[c, k : k + 1, :] for c in range(2)]
                below = [t[c, k + 1, rows, :] for c in range(2)] if k + 1 < nlev else None
                hu = 0.5 * u[k, rows, :].astype(f32)
                hv = 0.5 * v[k, rows, :].astype(f32)
                for ref, where, value in pending:
                    ref[where] = value
                pending = []
                s = side[k]
                in_e, in_n = lev_e > k, lev_n > k
                pe, qe = jnp.where(in_e, hu + s, 0.0), jnp.where(in_e, hu - s, 0.0)
                pn, qn = jnp.where(in_n, hv + s, 0.0), jnp.where(in_n, hv - s, 0.0)
                wet = lev > k
                if k + 1 < nlev:
                    fall_w = jnp.where(lev > k + 1, vert[k], 0.0)
                for c in range(2):
                    x = here[c]
                    up = jnp.where(sub_c == CHUNK - 1, top[c], pltpu.roll(x, CHUNK - 1, 0))
                    east = pe * x + qe * pltpu.roll(x, nx - 1, 1)
                    north = pn * x + qn * up
                    south = jnp.where(sub_c == 0, under[c], pltpu.roll(north, 1, 0))
                    place = 32 * c + k
                    lf = pltpu.roll(from_lf, LANES - place, 1) if place else from_lf
                    rt = pltpu.roll(from_rt, LANES - 1 - place, 1)
                    shared = jnp.concatenate(
                        [jnp.where(lane_t == 0, lf, 0.0)]
                        + [jnp.zeros((CHUNK, LANES), f32)] * (nx // LANES - 2)
                        + [jnp.where(lane_t == LANES - 1, -rt, 0.0)],
                        axis=1,
                    )
                    new = x + (pltpu.roll(east, 1, 1) - east + shared) + (south - north) - falls[c]
                    if k + 1 < nlev:
                        falls[c] = fall_w * (below[c] - x)
                        new = new + falls[c]
                    pending.append((o, (c, k, rows), jnp.where(wet, new, 0.0)))
                    pending.append((flx, (c, slice(k, k + 1)), north[CHUNK - 1 :]))
            for ref, where, value in pending:
                ref[where] = value
            for c in range(2):
                fall_in[c, rows, :] = falls[c]
            return 0

        lax.fori_loop(0, ny // CHUNK, rows_of, 0)
        span = pl.ds(first, end - first)
        for c, dst in enumerate((o1h, o2h)):
            ends = [o[c, k, ny - 1 : ny, :] - rows_up[c, k : k + 1, :] for k in range(first, end)]
            for k in range(first, end):
                o[c, k, ny - 1 : ny, :] = ends[k - first]
            copy = pltpu.make_async_copy(o.at[c, span], dst.at[span], out_sem.at[len(outs)])
            copy.start()
            outs.append(copy)

    tracer_pass(0, SPLIT)

    sub8 = lax.broadcasted_iota(jnp.int32, (8, nx), 0) < 4
    sub8c = sub8[:, :LANES]
    lane8 = lax.broadcasted_iota(jnp.int32, (8, LANES), 1) < 64
    row = lax.broadcasted_iota(jnp.int32, (ny + 8, nx + LANES), 0)
    mask = jnp.where(row < ny, 1.0, jnp.where(row < ny + 4, up_ok, dn_ok)).astype(f32)

    def widened(n):
        pieces = []
        for g in range(ny // 8):
            right = pltpu.roll(h_rt[n], LANES - WIDE * g, 1) if g else h_rt[n]
            shift = (LANES - WIDE - WIDE * g) % LANES
            left = pltpu.roll(h_lf[n], shift, 1) if shift else h_lf[n]
            pieces.append(jnp.where(lane8, right, left))
        beside = jnp.concatenate(pieces, axis=0)
        ends = jnp.where(sub8, h_up[n], h_dn[n])
        corner = jnp.where(
            sub8c, jnp.where(lane8, h_cn[3, n], h_cn[2, n]), jnp.where(lane8, h_cn[1, n], h_cn[0, n])
        )
        top = jnp.concatenate([fld[n], beside], axis=1)
        bottom = jnp.concatenate([ends, corner], axis=1)
        return jnp.concatenate([top, bottom], axis=0) * mask

    for copy in rim_fixed:
        copy.wait_recv()
    depth, diag = widened(1), widened(2)
    for copy in rim_force:
        copy.wait_recv()
    tall, wide = ny + 8, nx + LANES

    def operate(a):
        b = pltpu.roll(a, wide - 1, 1)
        cc = pltpu.roll(a, tall - 1, 0)
        d = pltpu.roll(b, tall - 1, 0)
        p = depth * (d - a)
        q = depth * (b - cc)
        return (diag * a - p + pltpu.roll(q, 1, 1) + pltpu.roll(pltpu.roll(p, 1, 1) - q, 1, 0)) * mask

    def moment(a, b):
        prod = a[:ny, :nx] * b[:ny, :nx]
        prod = jnp.sum(prod.reshape(ny // 8, 8, nx), axis=0)
        prod = sum(prod[:, n : n + LANES] for n in range(0, nx, LANES))
        return jnp.sum(prod, axis=0, keepdims=True)

    w0 = widened(0)
    w1 = operate(w0)
    w2 = operate(w1)
    w3 = operate(w2)
    v1r[...] = w1[:ny, :nx]
    v2r[...] = w2[:ny, :nx]
    pairs = ((w0, w0), (w0, w1), (w1, w1), (w1, w2), (w2, w2), (w2, w3))
    mom[...] = jnp.concatenate([moment(a, b) for a, b in pairs] + [jnp.zeros((2, LANES), f32)], axis=0)

    for dy, dx in column:
        send(mom, gath_by.at[by], gsend.at[0], grecv.at[0], neighbour(dy, dx))
    gath_by[by] = mom[...]
    tracer_pass(SPLIT, SECOND)
    rest = gath_by.at[pl.ds(0, nby - 1)]
    pltpu.make_async_copy(rest, rest, grecv.at[0]).wait()
    part[...] = jnp.sum(gath_by[...], axis=0)
    for dy, dx in line:
        send(part, gath.at[bx], gsend.at[1], grecv.at[1], neighbour(dy, dx))
    gath[bx] = part[...]
    tracer_pass(SECOND, nlev)
    for copy in edge + rim_fixed + rim_force:
        copy.wait_send()
    every = gath.at[pl.ds(0, nbx - 1)]
    pltpu.make_async_copy(every, every, grecv.at[1]).wait()
    whole = jnp.sum(jnp.sum(gath[...], axis=0), axis=1, keepdims=True)
    moments = [jnp.broadcast_to(whole[n : n + 1], (8, LANES)) for n in range(6)]
    weights = [jnp.concatenate([x] * (nx // LANES), axis=1) for x in iterate_weights(moments)]
    for r in range(0, ny, 8):
        rows = slice(r, r + 8)
        surf[rows, :] = weights[0] * fld[0, rows, :] + weights[1] * v1r[rows, :] + weights[2] * v2r[rows, :]
    pltpu.make_async_copy(rest, rest, gsend.at[0]).wait()
    pltpu.make_async_copy(every, every, gsend.at[1]).wait()
    for copy in outs:
        copy.wait()


def on_device(nby, nbx, t1, t2, u, v, lev, side, vert, thick, cd, dg):
    nlev, ny, nx = t1.shape
    anywhere = pl.BlockSpec(memory_space=pl.ANY)
    vmem = pltpu.VMEM
    dma = pltpu.SemaphoreType.DMA
    cells = nlev * ny * nx
    made = pl.pallas_call(
        functools.partial(kernel, nby, nbx, nlev),
        out_shape=(
            jax.ShapeDtypeStruct(t1.shape, f32),
            jax.ShapeDtypeStruct(t1.shape, f32),
            jax.ShapeDtypeStruct((ny, nx), f32),
        ),
        in_specs=[anywhere] * 10,
        out_specs=(anywhere, anywhere, pl.BlockSpec(memory_space=vmem)),
        scratch_shapes=[pltpu.SMEM((nlev,), f32)] * 3
        + [
            vmem((2, nlev, ny, nx), f32),
            vmem((nlev, ny, nx), u.dtype),
            vmem((nlev, ny, nx), v.dtype),
            vmem((ny, nx), jnp.int32),
            vmem((2, nlev, ny, nx), f32),
            vmem((80, nx), f32),
            vmem((56, nx), f32),
            vmem((80, nx), f32),
            vmem((56, nx), f32),
            vmem((ny, LANES), f32),
            vmem((ny, LANES), f32),
            vmem((ny, LANES), f32),
            vmem((ny, LANES), f32),
            vmem((3, ny, nx), f32),
            vmem((3, ny, nx), f32),
            vmem((2, ny, nx), f32),
            vmem((2, 24, nx), f32),
            vmem((2, 24, nx), f32),
            vmem((2, ny, LANES), f32),
            vmem((3, ny, nx), f32),
            vmem((3, 8, nx), f32),
            vmem((3, 8, nx), f32),
            vmem((3, 8, LANES), f32),
            vmem((3, 8, LANES), f32),
            vmem((2, 3, 8, LANES), f32),
            vmem((4, 3, 8, LANES), f32),
            vmem((ny, nx), f32),
            vmem((ny, nx), f32),
            vmem((8, LANES), f32),
            vmem((8, LANES), f32),
            vmem((nby, 8, LANES), f32),
            vmem((nbx, 8, LANES), f32),
            dma((14,)),
            dma((6,)),
            dma((4,)),
            dma((4,)),
            dma((8,)),
            dma((8,)),
            dma((8,)),
            dma((8,)),
            dma((2,)),
            dma((2,)),
        ],
        compiler_params=pltpu.CompilerParams(
            collective_id=0, has_side_effects=True, vmem_limit_bytes=VMEM_MIB * 2**20
        ),
        cost_estimate=pl.CostEstimate(flops=60 * cells, bytes_accessed=20 * cells, transcendentals=0),
    )(side, vert, thick, t1, t2, u, v, lev, cd, dg)

    return pl.pallas_call(
        hand_on,
        out_shape=tuple(jax.ShapeDtypeStruct(x.shape, x.dtype) for x in made),
        in_specs=[anywhere] * 3,
        out_specs=(anywhere,) * 3,
        scratch_shapes=[vmem((2, nlev, ny, nx), f32), vmem((ny, nx), f32), dma((2, 2 * PARTS + 1))],
        compiler_params=pltpu.CompilerParams(vmem_limit_bytes=VMEM_MIB * 2**20),
        cost_estimate=pl.CostEstimate(flops=0, bytes_accessed=16 * cells, transcendentals=0),
    )(*made)


def hand_on(a, b, c, a_out, b_out, c_out, stage, plane, sems):
    step = a.shape[0] // PARTS
    moves = [(c, plane, c_out)]
    for n in range(PARTS):
        span = pl.ds(n * step, step)
        moves.append((a.at[span], stage.at[0, span], a_out.at[span]))
        moves.append((b.at[span], stage.at[1, span], b_out.at[span]))
    ins = [pltpu.make_async_copy(src, via, sems.at[0, n]) for n, (src, via, _) in enumerate(moves)]
    outs = [pltpu.make_async_copy(via, dst, sems.at[1, n]) for n, (_, via, dst) in enumerate(moves)]
    for copy in ins:
        copy.start()
    for come, go in zip(ins, outs):
        come.wait()
        go.start()
    for copy in outs:
        copy.wait()


def solution(mesh):
    def body(t1, t2, u, v, lev, side, vert, thick, cd, dg):
        return on_device(mesh.shape["by"], mesh.shape["bx"], t1, t2, u, v, lev, side, vert, thick, cd, dg)

    block, plane = P(None, "by", "bx"), P("by", "bx")
    return jax.shard_map(
        body,
        mesh=mesh,
        in_specs=(block, block, block, block, plane, P(), P(), P(), plane, plane),
        out_specs=(block, block, plane),
        check_vma=False,
    )
```

```python
import functools

import jax
import jax.numpy as jnp
from jax import lax
from jax.experimental import pallas as pl
from jax.experimental.pallas import tpu as pltpu
from jax.sharding import PartitionSpec as P

ITERS = 3
SHIFT = 3.0
CHUNK = 16
WIDE = 16
PARTS = 3
EARLY = 6
SPLIT = 8
VMEM_MIB = 62
LANES = 128
MESH = pl.DeviceIdType.MESH
f32 = jnp.float32
SIDES = ((1, 0), (-1, 0), (0, 1), (0, -1), (1, 1), (1, -1), (-1, 1), (-1, -1))


def iterate_weights(moments):
    def add(a, b, scale):
        longer = max(len(a), len(b))
        out = []
        for n in range(longer):
            if n >= len(a):
                out.append(scale * b[n])
            elif n >= len(b):
                out.append(a[n])
            else:
                out.append(a[n] + scale * b[n])
        return out

    def operate(a):
        shifted = [SHIFT * x for x in a] + [None]
        for n, x in enumerate(a):
            shifted[n + 1] = x if shifted[n + 1] is None else shifted[n + 1] + x
        return shifted

    def dot(a, b):
        total = None
        for i, x in enumerate(a):
            for j, y in enumerate(b):
                term = x * y * moments[i + j]
                total = term if total is None else total + term
        return total

    residual = [jnp.ones_like(moments[0])]
    image = operate(residual)
    now = dot(residual, residual)
    alpha = now / dot(residual, image)
    direction, along = residual, image
    surface = [jnp.zeros_like(moments[0])]
    for step in range(ITERS):
        surface = add(surface, direction, alpha)
        if step + 1 < ITERS:
            residual = add(residual, along, -alpha)
            image = operate(residual)
            new = dot(residual, residual)
            product = dot(residual, image)
            ratio = new / now
            alpha = new / (product - ratio * new / alpha)
            direction = add(residual, direction, ratio)
            along = add(image, along, ratio)
            now = new
    return surface


def kernel(
    nby, nbx, nlev,
    sideh, verth, thickh, t1h, t2h, uh, vh, levh, cdh, dgh,
    o1h, o2h, surf,
    side, vert, thick, t, u, v, levi, o, row_up, row_dn, got_dn, got_up, col_rt, col_lf, got_lf, got_rt,
    lv, sums, fall_in, flx, rows_up, cols, fld, h_up, h_dn, h_rt, h_lf, narrow, h_cn, v1r, v2r, mom, gath,
    load_sem, out_sem, send_a, recv_a, send_b, recv_b, send_c, recv_c, gsend, grecv,
):
    by, bx = lax.axis_index("by"), lax.axis_index("bx")
    total = nby * nbx
    me = by * nbx + bx
    ny, nx = fld.shape[1], fld.shape[2]

    def neighbour(dy, dx):
        y, x = by + dy % nby, bx + dx % nbx
        return (jnp.where(y >= nby, y - nby, y), jnp.where(x >= nbx, x - nbx, x))

    others = [(dy, dx) for dy in range(nby) for dx in range(nbx)][1:]
    barrier = pltpu.get_barrier_semaphore()
    for dy, dx in others:
        pl.semaphore_signal(barrier, inc=1, device_id=neighbour(dy, dx), device_id_type=MESH)

    loads = [
        pltpu.make_async_copy(sideh, side, load_sem.at[8]),
        pltpu.make_async_copy(verth, vert, load_sem.at[9]),
        pltpu.make_async_copy(thickh, thick, load_sem.at[10]),
        pltpu.make_async_copy(levh, levi, load_sem.at[11]),
    ]
    groups = ((0, EARLY), (EARLY, nlev))
    bulk = []
    for g, (first, end) in enumerate(groups):
        span = pl.ds(first, end - first)
        bulk.append([
            pltpu.make_async_copy(t1h.at[span], t.at[0, span], load_sem.at[4 * g]),
            pltpu.make_async_copy(t2h.at[span], t.at[1, span], load_sem.at[4 * g + 1]),
            pltpu.make_async_copy(uh.at[span], u.at[span], load_sem.at[4 * g + 2]),
            pltpu.make_async_copy(vh.at[span], v.at[span], load_sem.at[4 * g + 3]),
        ])
    planes = [
        pltpu.make_async_copy(cdh, fld.at[1], load_sem.at[12]),
        pltpu.make_async_copy(dgh, fld.at[2], load_sem.at[13]),
    ]
    for copy in loads + bulk[0] + bulk[1] + planes:
        copy.start()

    up_ok = jnp.where(by < nby - 1, 1.0, 0.0).astype(f32)
    dn_ok = jnp.where(by > 0, 1.0, 0.0).astype(f32)

    for copy in loads:
        copy.wait()
    levels = levi[...]
    levf = levels.astype(f32)

    sub_c = lax.broadcasted_iota(jnp.int32, (CHUNK, nx), 0)
    lane_c = lax.broadcasted_iota(jnp.int32, (CHUNK, nx), 1)
    for r in range(0, ny, CHUNK):
        rows = slice(r, r + CHUNK)
        lev = levf[rows]
        lev_rt = jnp.where(lane_c == nx - 1, 0.0, pltpu.roll(lev, nx - 1, 1))
        above = levf[r + CHUNK : r + CHUNK + 1] if r + CHUNK < ny else 0.0
        lev_up = jnp.where(sub_c == CHUNK - 1, above, pltpu.roll(lev, CHUNK - 1, 0))
        lv[0, rows, :] = lev
        lv[1, rows, :] = jnp.minimum(lev, lev_rt)
        lv[2, rows, :] = jnp.minimum(lev, lev_up)
    def force_pass(g):
        start, end = groups[g]

        def rows_of(n, _):
            r = pl.multiple_of(n * CHUNK, CHUNK)
            rows = pl.ds(r, CHUNK)
            above = jnp.minimum(r + CHUNK, ny - 1)
            lev, lev_e, lev_n = lv[0, rows, :], lv[1, rows, :], lv[2, rows, :]
            before = None
            if start:
                before = t[0, start - 1, rows, :] - 0.5 * t[1, start - 1, rows, :]
                acc = [sums[m, rows, :] for m in range(3)]
            else:
                acc = [jnp.zeros((CHUNK, nx), f32)] * 3
            for k in range(start, end):
                g_here = t[0, k, rows, :] - 0.5 * t[1, k, rows, :]
                top = t[0, k, pl.ds(above, 1), :] - 0.5 * t[1, k, pl.ds(above, 1), :]
                g_up = jnp.where(sub_c == CHUNK - 1, top, pltpu.roll(g_here, CHUNK - 1, 0))
                g_rt = pltpu.roll(g_here, nx - 1, 1)
                twice = 2.0 * side[k]
                east = u[k, rows, :].astype(f32) * (g_here + g_rt) - twice * (g_rt - g_here)
                north = v[k, rows, :].astype(f32) * (g_here + g_up) - twice * (g_up - g_here)
                inside = thick[k] * g_here
                if k:
                    inside = inside + (vert[k - 1] * (thick[k - 1] - thick[k])) * (g_here - before)
                half = 0.5 * thick[k]
                acc[0] = acc[0] + jnp.where(lev > k, inside, 0.0)
                acc[1] = acc[1] + half * jnp.where(lev_e > k, east, 0.0)
                acc[2] = acc[2] + half * jnp.where(lev_n > k, north, 0.0)
                before = g_here
            for m in range(3):
                sums[m, rows, :] = acc[m]
            return 0

        lax.fori_loop(0, ny // CHUNK, rows_of, 0)

    for copy in bulk[0] + bulk[1]:
        copy.wait()

    lane = lax.broadcasted_iota(jnp.int32, (ny, LANES), 1)
    row_up[pl.ds(48, 8), :] = jnp.broadcast_to(levf[ny - 1 : ny], (8, nx))
    row_dn[pl.ds(48, 8), :] = jnp.broadcast_to(levf[0:1], (8, nx))
    right = jnp.where(lane == 96, pltpu.roll(levf[:, nx - LANES :], 97, 1), 0.0)
    left = jnp.where(lane == 96, pltpu.roll(levf[:, :LANES], 96, 1), 0.0)
    for c in range(2):
        for k in range(nlev):
            place = 32 * c + k
            right = jnp.where(lane == place, pltpu.roll(t[c, k, :, nx - LANES :], place + 1, 1), right)
            tile = t[c, k, :, :LANES]
            left = jnp.where(lane == place, pltpu.roll(tile, place, 1) if place else tile, left)
    for k in range(nlev):
        right = jnp.where(lane == 64 + k, pltpu.roll(u[k, :, nx - LANES :].astype(f32), 65 + k, 1), right)
    for c in range(2):
        upper = [t[c, k, ny - 1 : ny, :] for k in range(nlev)]
        lower = [t[c, k, 0:1, :] for k in range(nlev)]
        for k in range(nlev):
            row_up[24 * c + k : 24 * c + k + 1, :] = upper[k]
            row_dn[24 * c + k : 24 * c + k + 1, :] = lower[k]
    upper = [v[k, ny - 16 :, :].astype(f32)[15:16] for k in range(nlev)]
    for k in range(nlev):
        row_up[56 + k : 57 + k, :] = upper[k]
    col_rt[...] = right
    col_lf[...] = left

    pl.semaphore_wait(barrier, total - 1)

    def send(src, dst, ssem, rsem, to):
        copy = pltpu.make_async_remote_copy(
            src_ref=src, dst_ref=dst, send_sem=ssem, recv_sem=rsem, device_id=to, device_id_type=MESH
        )
        copy.start()
        return copy

    edge = [
        send(row_up, got_dn, send_a.at[0], recv_a.at[0], neighbour(1, 0)),
        send(row_dn, got_up, send_a.at[1], recv_a.at[1], neighbour(-1, 0)),
        send(col_rt, got_lf, send_a.at[2], recv_a.at[2], neighbour(0, 1)),
        send(col_lf, got_rt, send_a.at[3], recv_a.at[3], neighbour(0, -1)),
    ]

    lane_8 = lane[:8]

    def fold(n):
        right = left = jnp.zeros((8, LANES), f32)
        for g in range(ny // 8):
            rows = slice(8 * g, 8 * g + 8)
            mine = (lane_8 >= WIDE * g) & (lane_8 < WIDE * g + WIDE)
            right = jnp.where(mine, pltpu.roll(fld[n, rows, nx - LANES :], (WIDE * g + WIDE) % LANES, 1), right)
            tile = fld[n, rows, :LANES]
            left = jnp.where(mine, pltpu.roll(tile, WIDE * g, 1) if g else tile, left)
        narrow[0, n] = right
        narrow[1, n] = left

    def rim(which, ssem, rsem):
        copies = []
        for n, (dy, dx) in enumerate(SIDES):
            rows = pl.ds(ny - 8, 8) if dy > 0 else pl.ds(0, 8)
            cols = pl.ds(0, nx) if dx == 0 else (pl.ds(nx - LANES, LANES) if dx > 0 else pl.ds(0, LANES))
            place = {0: h_dn, 1: h_up, 2: h_lf, 3: h_rt}.get(n)
            dst = h_cn.at[n - 4, which] if place is None else place.at[which]
            src = fld.at[which, rows, cols] if dy else narrow.at[n - 2, which]
            copies.append(send(src, dst, ssem.at[n], rsem.at[n], neighbour(dy, dx)))
        return copies

    for copy in planes:
        copy.wait()
    fld[1] = fld[1] * jnp.where(levels > 0, 0.5, 0.0).astype(f32)
    fld[2] = fld[2] - SHIFT
    fold(1)
    fold(2)
    rim_fixed = rim(pl.ds(1, 2), send_b, recv_b)

    force_pass(0)
    force_pass(1)
    force = sums[0] + (pltpu.roll(sums[1], 1, 1) - sums[1]) + (pltpu.roll(sums[2], 1, 0) - sums[2])
    fld[0] = force

    k_sub = lax.broadcasted_iota(jnp.int32, (24, nx), 0)
    k_lane = lax.rem(lane, 32)
    side_sub = jnp.zeros((24, nx), f32)
    thick_sub = jnp.zeros((24, nx), f32)
    side_lane = jnp.zeros((8, LANES), f32)
    thick_lane = jnp.zeros((8, LANES), f32)
    for k in range(nlev):
        side_sub = jnp.where(k_sub == k, side[k], side_sub)
        thick_sub = jnp.where(k_sub == k, thick[k], thick_sub)
        side_lane = jnp.where(k_lane[:8] == k, side[k], side_lane)
        thick_lane = jnp.where(lane[:8] == k, thick[k], thick_lane)
        thick_lane = jnp.where(lane[:8] == 32 + k, -0.5 * thick[k], thick_lane)
    side_lane, thick_lane = (jnp.concatenate([x] * (ny // 8), axis=0) for x in (side_lane, thick_lane))

    for copy in edge:
        copy.wait_recv()

    def row_flux(lower, upper, ok):
        lowest = jnp.minimum(lower[48:49, :], upper[48:49, :]) * ok
        is_open = k_sub.astype(f32) < lowest
        half = 0.5 * lower[56:80, :]
        p, q = jnp.where(is_open, half + side_sub, 0.0), jnp.where(is_open, half - side_sub, 0.0)
        out = []
        for c in range(2):
            flux = p * lower[24 * c : 24 * c + 24, :] + q * upper[24 * c : 24 * c + 24, :]
            out.append(jnp.where(is_open, flux, 0.0))
        return out

    def col_flux(came, beyond):
        half = 0.5 * jnp.where(lane < 32, pltpu.roll(came, 64, 1), pltpu.roll(came, 96, 1))
        lowest = jnp.minimum(came[:, 96:97], beyond[:, 96:97])
        flux = (half + side_lane) * came + (half - side_lane) * beyond
        return jnp.where(k_lane.astype(f32) < lowest, flux, 0.0)

    flux_dn = row_flux(got_dn, row_dn, dn_ok)
    flux_up = row_flux(row_up, got_up, up_ok)
    flux_lf = col_flux(got_lf[...], col_lf[...])
    flux_rt = col_flux(col_rt[...], got_rt[...])

    def weighed(flux):
        return jnp.sum(thick_sub * (flux[0] - 0.5 * flux[1]), axis=0, keepdims=True)

    fld[0, 0:1, :] += weighed(flux_dn)
    fld[0, ny - 1 : ny, :] -= weighed(flux_up)
    fld[0, :, :LANES] += jnp.where(lane == 0, jnp.sum(thick_lane * flux_lf, axis=1, keepdims=True), 0.0)
    fld[0, :, nx - LANES :] -= jnp.where(lane == LANES - 1, jnp.sum(thick_lane * flux_rt, axis=1, keepdims=True), 0.0)
    fold(0)
    rim_force = rim(0, send_c, recv_c)

    outs = []
    for c in range(2):
        flx[c] = flux_dn[c]
        rows_up[c] = flux_up[c]
    cols[0] = flux_lf
    cols[1] = flux_rt
    fall_in[...] = jnp.zeros_like(fall_in)
    lane_t = lane[:CHUNK]

    def tracer_pass(first, end):
        def rows_of(n, _):
            r = pl.multiple_of(n * CHUNK, CHUNK)
            rows = pl.ds(r, CHUNK)
            above = jnp.minimum(r + CHUNK, ny - 1)
            lev, lev_e, lev_n = lv[0, rows, :], lv[1, rows, :], lv[2, rows, :]
            from_lf, from_rt = cols[0, rows, :], cols[1, rows, :]
            falls = [fall_in[c, rows, :] for c in range(2)]
            pending = []
            for k in range(first, end):
                here = [t[c, k, rows, :] for c in range(2)]
                top = [t[c, k, pl.ds(above, 1), :] for c in range(2)]
                under = [flx[c, k : k + 1, :] for c in range(2)]
                below = [t[c, k + 1, rows, :] for c in range(2)] if k + 1 < nlev else None
                hu = 0.5 * u[k, rows, :].astype(f32)
                hv = 0.5 * v[k, rows, :].astype(f32)
                for ref, where, value in pending:
                    ref[where] = value
                pending = []
                s = side[k]
                in_e, in_n = lev_e > k, lev_n > k
                pe, qe = jnp.where(in_e, hu + s, 0.0), jnp.where(in_e, hu - s, 0.0)
                pn, qn = jnp.where(in_n, hv + s, 0.0), jnp.where(in_n, hv - s, 0.0)
                wet = lev > k
                if k + 1 < nlev:
                    fall_w = jnp.where(lev > k + 1, vert[k], 0.0)
                for c in range(2):
                    x = here[c]
                    up = jnp.where(sub_c == CHUNK - 1, top[c], pltpu.roll(x, CHUNK - 1, 0))
                    east = pe * x + qe * pltpu.roll(x, nx - 1, 1)
                    north = pn * x + qn * up
                    south = jnp.where(sub_c == 0, under[c], pltpu.roll(north, 1, 0))
                    place = 32 * c + k
                    lf = pltpu.roll(from_lf, LANES - place, 1) if place else from_lf
                    rt = pltpu.roll(from_rt, LANES - 1 - place, 1)
                    shared = jnp.concatenate(
                        [jnp.where(lane_t == 0, lf, 0.0)]
                        + [jnp.zeros((CHUNK, LANES), f32)] * (nx // LANES - 2)
                        + [jnp.where(lane_t == LANES - 1, -rt, 0.0)],
                        axis=1,
                    )
                    new = x + (pltpu.roll(east, 1, 1) - east + shared) + (south - north) - falls[c]
                    if k + 1 < nlev:
                        falls[c] = fall_w * (below[c] - x)
                        new = new + falls[c]
                    pending.append((o, (c, k, rows), jnp.where(wet, new, 0.0)))
                    pending.append((flx, (c, slice(k, k + 1)), north[CHUNK - 1 :]))
            for ref, where, value in pending:
                ref[where] = value
            for c in range(2):
                fall_in[c, rows, :] = falls[c]
            return 0

        lax.fori_loop(0, ny // CHUNK, rows_of, 0)
        span = pl.ds(first, end - first)
        for c, dst in enumerate((o1h, o2h)):
            ends = [o[c, k, ny - 1 : ny, :] - rows_up[c, k : k + 1, :] for k in range(first, end)]
            for k in range(first, end):
                o[c, k, ny - 1 : ny, :] = ends[k - first]
            copy = pltpu.make_async_copy(o.at[c, span], dst.at[span], out_sem.at[len(outs)])
            copy.start()
            outs.append(copy)

    tracer_pass(0, SPLIT)

    sub8 = lax.broadcasted_iota(jnp.int32, (8, nx), 0) < 4
    sub8c = sub8[:, :LANES]
    lane8 = lax.broadcasted_iota(jnp.int32, (8, LANES), 1) < 64
    row = lax.broadcasted_iota(jnp.int32, (ny + 8, nx + LANES), 0)
    mask = jnp.where(row < ny, 1.0, jnp.where(row < ny + 4, up_ok, dn_ok)).astype(f32)

    def widened(n):
        pieces = []
        for g in range(ny // 8):
            right = pltpu.roll(h_rt[n], LANES - WIDE * g, 1) if g else h_rt[n]
            shift = (LANES - WIDE - WIDE * g) % LANES
            left = pltpu.roll(h_lf[n], shift, 1) if shift else h_lf[n]
            pieces.append(jnp.where(lane8, right, left))
        beside = jnp.concatenate(pieces, axis=0)
        ends = jnp.where(sub8, h_up[n], h_dn[n])
        corner = jnp.where(
            sub8c, jnp.where(lane8, h_cn[3, n], h_cn[2, n]), jnp.where(lane8, h_cn[1, n], h_cn[0, n])
        )
        top = jnp.concatenate([fld[n], beside], axis=1)
        bottom = jnp.concatenate([ends, corner], axis=1)
        return jnp.concatenate([top, bottom], axis=0) * mask

    for copy in rim_fixed:
        copy.wait_recv()
    depth, diag = widened(1), widened(2)
    for copy in rim_force:
        copy.wait_recv()
    tall, wide = ny + 8, nx + LANES

    def operate(a):
        b = pltpu.roll(a, wide - 1, 1)
        cc = pltpu.roll(a, tall - 1, 0)
        d = pltpu.roll(b, tall - 1, 0)
        p = depth * (d - a)
        q = depth * (b - cc)
        return (diag * a - p + pltpu.roll(q, 1, 1) + pltpu.roll(pltpu.roll(p, 1, 1) - q, 1, 0)) * mask

    def moment(a, b):
        prod = a[:ny, :nx] * b[:ny, :nx]
        prod = jnp.sum(prod.reshape(ny // 8, 8, nx), axis=0)
        prod = sum(prod[:, n : n + LANES] for n in range(0, nx, LANES))
        return jnp.sum(prod, axis=0, keepdims=True)

    w0 = widened(0)
    w1 = operate(w0)
    w2 = operate(w1)
    w3 = operate(w2)
    v1r[...] = w1[:ny, :nx]
    v2r[...] = w2[:ny, :nx]
    pairs = ((w0, w0), (w0, w1), (w1, w1), (w1, w2), (w2, w2), (w2, w3))
    mom[...] = jnp.concatenate([moment(a, b) for a, b in pairs] + [jnp.zeros((2, LANES), f32)], axis=0)

    for dy, dx in others:
        send(mom, gath.at[me], gsend, grecv, neighbour(dy, dx))
    gath[me] = mom[...]
    tracer_pass(SPLIT, nlev)
    for copy in edge + rim_fixed + rim_force:
        copy.wait_send()
    for copy in outs:
        copy.wait()
    every = gath.at[pl.ds(0, total - 1)]
    pltpu.make_async_copy(every, every, grecv).wait()
    whole = jnp.sum(jnp.sum(gath[...], axis=0), axis=1, keepdims=True)
    moments = [jnp.broadcast_to(whole[n : n + 1], (8, LANES)) for n in range(6)]
    weights = [jnp.concatenate([x] * (nx // LANES), axis=1) for x in iterate_weights(moments)]
    for r in range(0, ny, 8):
        rows = slice(r, r + 8)
        surf[rows, :] = weights[0] * fld[0, rows, :] + weights[1] * v1r[rows, :] + weights[2] * v2r[rows, :]
    pltpu.make_async_copy(every, every, gsend).wait()


def on_device(nby, nbx, t1, t2, u, v, lev, side, vert, thick, cd, dg):
    nlev, ny, nx = t1.shape
    anywhere = pl.BlockSpec(memory_space=pl.ANY)
    vmem = pltpu.VMEM
    dma = pltpu.SemaphoreType.DMA
    cells = nlev * ny * nx
    made = pl.pallas_call(
        functools.partial(kernel, nby, nbx, nlev),
        out_shape=(
            jax.ShapeDtypeStruct(t1.shape, f32),
            jax.ShapeDtypeStruct(t1.shape, f32),
            jax.ShapeDtypeStruct((ny, nx), f32),
        ),
        in_specs=[anywhere] * 10,
        out_specs=(anywhere, anywhere, pl.BlockSpec(memory_space=vmem)),
        scratch_shapes=[pltpu.SMEM((nlev,), f32)] * 3
        + [
            vmem((2, nlev, ny, nx), f32),
            vmem((nlev, ny, nx), u.dtype),
            vmem((nlev, ny, nx), v.dtype),
            vmem((ny, nx), jnp.int32),
            vmem((2, nlev, ny, nx), f32),
            vmem((80, nx), f32),
            vmem((56, nx), f32),
            vmem((80, nx), f32),
            vmem((56, nx), f32),
            vmem((ny, LANES), f32),
            vmem((ny, LANES), f32),
            vmem((ny, LANES), f32),
            vmem((ny, LANES), f32),
            vmem((3, ny, nx), f32),
            vmem((3, ny, nx), f32),
            vmem((2, ny, nx), f32),
            vmem((2, 24, nx), f32),
            vmem((2, 24, nx), f32),
            vmem((2, ny, LANES), f32),
            vmem((3, ny, nx), f32),
            vmem((3, 8, nx), f32),
            vmem((3, 8, nx), f32),
            vmem((3, 8, LANES), f32),
            vmem((3, 8, LANES), f32),
            vmem((2, 3, 8, LANES), f32),
            vmem((4, 3, 8, LANES), f32),
            vmem((ny, nx), f32),
            vmem((ny, nx), f32),
            vmem((8, LANES), f32),
            vmem((nby * nbx, 8, LANES), f32),
            dma((14,)),
            dma((4,)),
            dma((4,)),
            dma((4,)),
            dma((8,)),
            dma((8,)),
            dma((8,)),
            dma((8,)),
            dma,
            dma,
        ],
        compiler_params=pltpu.CompilerParams(
            collective_id=0, has_side_effects=True, vmem_limit_bytes=VMEM_MIB * 2**20
        ),
        cost_estimate=pl.CostEstimate(flops=60 * cells, bytes_accessed=20 * cells, transcendentals=0),
    )(side, vert, thick, t1, t2, u, v, lev, cd, dg)

    return pl.pallas_call(
        hand_on,
        out_shape=tuple(jax.ShapeDtypeStruct(x.shape, x.dtype) for x in made),
        in_specs=[anywhere] * 3,
        out_specs=(anywhere,) * 3,
        scratch_shapes=[vmem((2, nlev, ny, nx), f32), vmem((ny, nx), f32), dma((2, 2 * PARTS + 1))],
        compiler_params=pltpu.CompilerParams(vmem_limit_bytes=VMEM_MIB * 2**20),
        cost_estimate=pl.CostEstimate(flops=0, bytes_accessed=16 * cells, transcendentals=0),
    )(*made)


def hand_on(a, b, c, a_out, b_out, c_out, stage, plane, sems):
    step = a.shape[0] // PARTS
    moves = [(c, plane, c_out)]
    for n in range(PARTS):
        span = pl.ds(n * step, step)
        moves.append((a.at[span], stage.at[0, span], a_out.at[span]))
        moves.append((b.at[span], stage.at[1, span], b_out.at[span]))
    ins = [pltpu.make_async_copy(src, via, sems.at[0, n]) for n, (src, via, _) in enumerate(moves)]
    outs = [pltpu.make_async_copy(via, dst, sems.at[1, n]) for n, (_, via, dst) in enumerate(moves)]
    for copy in ins:
        copy.start()
    for come, go in zip(ins, outs):
        come.wait()
        go.start()
    for copy in outs:
        copy.wait()


def solution(mesh):
    def body(t1, t2, u, v, lev, side, vert, thick, cd, dg):
        return on_device(mesh.shape["by"], mesh.shape["bx"], t1, t2, u, v, lev, side, vert, thick, cd, dg)

    block, plane = P(None, "by", "bx"), P("by", "bx")
    return jax.shard_map(
        body,
        mesh=mesh,
        in_specs=(block, block, block, block, plane, P(), P(), P(), plane, plane),
        out_specs=(block, block, plane),
        check_vma=False,
    )
```
